128 devices in a mesh: tm: 32 (over x, z, core), row: 4 (over y).
Axes of the slice: x: 4, y: 4, z: 4, core: 2. Of those that a mesh axis runs over, the one named last changes fastest.
Arguments:
- gain_mats: bfloat16 [32, 1024, 1024], P('tm', 'row'), may hold values from -1 to 1
- offsets: bfloat16 [32, 1024], P('tm', 'row'), may hold values from -1.796875 to 1.796875
- spread_mats: bfloat16 [32, 1024, 1024], P('tm', 'row'), may hold values from -1 to 8, as said below
Outputs:
- smoothed_mean: bfloat16 [32, 1024], P('tm', 'row')
- smoothed_cov: bfloat16 [32, 1024, 1024], P('tm', 'row')
The draws below stay inside these ranges and needn't reach their ends.
Inputs may be any that keep to these rules, and one draw needn't show every extreme that they name: `spread_mats`: symmetric.
All inputs are finite; a program needn't handle non-finite values.
Results may differ from the reference program's by a relative error of at most 0.0035.
The reference program's roundings to bfloat16 on the way count: a program that leaves them out, or rounds other values in their place, can miss the bound.
Values may be sent and summed in bfloat16 or wider, within the bound.
A program may use at most 64 MiB of HBM per device.

```python
import jax
import jax.numpy as jnp
from jax import lax

D = 1024
STEPS = 32
LEVELS = 5


def draw_gain_mats(key, part):
    key = jax.random.fold_in(key, 11)
    key_rate, key_jitter, key_noise = jax.random.split(key, 3)
    low_rate, high_rate = (0.001, 0.3)
    rates = jnp.exp(jax.random.uniform(key_rate, (D,), jnp.float32, jnp.log(low_rate), jnp.log(high_rate)))
    jitter = jax.random.uniform(key_jitter, (STEPS, D), jnp.float32, 0.5, 2.0)
    diagonal = 0.995 * jnp.exp(-rates[None, :] * jitter)
    noise = jax.random.normal(key_noise, (STEPS, D, D), jnp.float32) * (0.05 / jnp.sqrt(D * 1.0))
    unit = jnp.eye(D, dtype=jnp.float32)
    return (noise * (1.0 - unit) + unit * diagonal[:, :, None]).astype(jnp.bfloat16)


def draw_spread_mats(key, part):
    key = jax.random.fold_in(key, 12)
    key_diag, key_noise = jax.random.split(key, 2)
    diagonal = jnp.exp(jax.random.uniform(key_diag, (STEPS, D), jnp.float32, jnp.log(0.1), jnp.log(1.0)))
    noise = jax.random.normal(key_noise, (STEPS, D, D), jnp.float32) * (0.08 / jnp.sqrt(2.0 * D))
    noise = noise + jnp.swapaxes(noise, 1, 2)
    unit = jnp.eye(D, dtype=jnp.float32)
    spread = noise * (1.0 - unit) + unit * diagonal[:, :, None]
    return spread.astype(jnp.bfloat16)


def block_scale(rng, dims, pieces, smallest, top_value):
    def one(axis_at, shards_of):
        heights = jax.random.uniform(jax.random.fold_in(jax.random.fold_in(rng, 6), axis_at), (shards_of,), jnp.float32, smallest / len(pieces), top_value / len(pieces))
        return jnp.repeat(jnp.exp(heights), dims[axis_at] // shards_of).reshape((-1,) + (1,) * (len(dims) - axis_at - 1))

    loudness = one(*pieces[0])
    for cut in pieces[1:]:
        loudness = loudness * one(*cut)
    return loudness


def scatter_about(rng, dims, scale, bound, cuts=(), kind=jnp.bfloat16):
    factor_of = block_scale(rng, dims, cuts, -0.22, 0.18) if cuts else 1.0
    entries = jax.random.normal(rng, dims, jnp.float32) * scale * factor_of
    return jnp.minimum(jnp.maximum(entries, -bound), bound).astype(kind)


def setup_inputs(seed: int = 0) -> dict:
    arg_keys = jax.random.split(jax.random.key(seed), 4)
    gain_mats = draw_gain_mats(jax.random.fold_in(arg_keys[3], 71), 0)
    offsets = scatter_about(arg_keys[1], (STEPS, D), 0.3, 1.796875, ((0, 32), (1, 4)))
    spread_mats = draw_spread_mats(jax.random.fold_in(arg_keys[3], 71), 0)
    return dict(gain_mats=gain_mats, offsets=offsets, spread_mats=spread_mats)


def mult(left, right):
    return jnp.dot(left.astype(jnp.float32), right.astype(jnp.float32), precision=lax.Precision.HIGHEST)


def combine(item):
    own_gain, own_offset, own_spread, far_gain, far_offset, far_spread = item
    new_gain = mult(own_gain, far_gain).astype(jnp.bfloat16)
    new_offset = (mult(own_gain, far_offset) + own_offset.astype(jnp.float32)).astype(jnp.bfloat16)
    middle = mult(own_gain, far_spread).astype(jnp.bfloat16)
    new_spread = (mult(middle, own_gain.T) + own_spread.astype(jnp.float32)).astype(jnp.bfloat16)
    return new_gain, new_offset, new_spread


def reference(gain_mats, offsets, spread_mats):
    gain = gain_mats.at[STEPS - 1].set(jnp.zeros((D, D), jnp.bfloat16))
    offset = offsets
    spread = spread_mats
    for level in range(LEVELS):
        distance = 2 ** level
        head = STEPS - distance
        new_gain, new_offset, new_spread = lax.map(combine, (gain[:head], offset[:head], spread[:head], gain[distance:], offset[distance:], spread[distance:]))
        gain = jnp.concatenate([new_gain, gain[head:]], axis=0)
        offset = jnp.concatenate([new_offset, offset[head:]], axis=0)
        spread = jnp.concatenate([new_spread, spread[head:]], axis=0)
    return offset, spread
```

```python
import functools

import jax
import jax.numpy as jnp
from jax import lax
from jax.experimental import pallas as pl
from jax.experimental.pallas import tpu as pltpu
from jax.sharding import PartitionSpec as P

MESH = pl.DeviceIdType.MESH
BF16 = jnp.bfloat16
F32 = jnp.float32
SLAB = 16


def dot(a, b):
    return jnp.dot(a, b, preferred_element_type=F32)


def dot_t(a, b):
    return lax.dot_general(a, b, (((1,), (1,)), ((), ())), preferred_element_type=F32)


def kernel(
    steps, levels, tile,
    e_in, g_in, l_in, o_g, o_l,
    e_first, e_later, far_e, far_lg, mid_out, mid_in, own_lg, acc_e,
    ring_s, ring_r, swap_s, swap_r, fe_s, fe_r, fl_s, fl_r, gg_s, gg_r, fg_s, fg_r,
):
    k = lax.axis_index("tm")
    r = lax.axis_index("row")
    right, opp, left = (lax.rem(r + o, 4) for o in (1, 2, 3))

    def at_row(row):
        return (k, row)

    def at_step(step):
        return (step, r)

    def copy(src, dst, ssem, rsem, dev):
        return pltpu.make_async_remote_copy(
            src_ref=src, dst_ref=dst, send_sem=ssem, recv_sem=rsem, device_id=dev, device_id_type=MESH
        )

    barrier = pltpu.get_barrier_semaphore()
    partners = [at_row(right), at_row(opp), at_row(left)]
    for s in range(levels):
        partners.append(at_step(lax.rem(k + 2**s, steps)))
        if 2 ** (s + 1) != steps:
            partners.append(at_step(lax.rem(k + steps - 2**s, steps)))
    for dev in partners:
        pl.semaphore_signal(barrier, inc=1, device_id=dev, device_id_type=MESH)

    def blocks(s):
        return e_first if s == 0 else e_later.at[s - 1]

    def gain(s, a, b):
        return e_first[a, b] if s == 0 else e_later[s - 1, b, a]

    def ring(s, way, slot, blk, h):
        ref = blocks(s).at[blk, pl.ds(2 * h, 2)]
        dev = at_row(right if way == 0 else left)
        return copy(ref, ref, ring_s.at[s, way, slot], ring_r.at[s, way, slot], dev)

    def ring_start(s):
        ring(s, 0, 0, r, 0).start()
        ring(s, 1, 1, r, 1).start()
        ring(s, 0, 1, r, 1).start()
        ring(s, 1, 0, r, 0).start()

    def ring_relay(s):
        ring(s, 0, 0, left, 0).wait_recv()
        ring(s, 0, 2, left, 0).start()
        ring(s, 1, 1, right, 1).wait_recv()
        ring(s, 1, 2, right, 1).start()

    def ring_near(s):
        ring(s, 0, 1, left, 1).wait_recv()
        ring(s, 1, 0, right, 0).wait_recv()

    def ring_opp(s):
        ring(s, 0, 2, opp, 0).wait_recv()
        ring(s, 1, 2, opp, 1).wait_recv()

    def ring_sent(s):
        for way in range(2):
            ring(s, way, 0, r, 0).wait_send()
            ring(s, way, 1, r, 1).wait_send()
        ring(s, 0, 2, left, 0).wait_send()
        ring(s, 1, 2, right, 1).wait_send()

    def far_gain_piece(blk):
        return copy(e_first.at[blk, r], far_e.at[0, blk], fe_s.at[0, blk], fe_r.at[0, blk], at_step(k - 1))

    def far_gain(s):
        return copy(e_later.at[s - 1, r], far_e.at[s], fe_s.at[s, 0], fe_r.at[s, 0], at_step(k - 2**s))

    def far_spread(s):
        if s == 0:
            part = own_lg.at[:, pl.ds(0, tile), :]
            there = far_lg.at[0, :, pl.ds(0, tile), :]
        else:
            part = own_lg
            there = far_lg.at[s]
        return copy(part, there, fl_s.at[s], fl_r.at[s], at_step(k - 2**s))

    def far_offset():
        return copy(
            own_lg.at[:, pl.ds(tile, SLAB), :], far_lg.at[0, :, pl.ds(tile, SLAB), :], fg_s, fg_r, at_step(k - 1)
        )

    def offset_piece(o):
        ref = own_lg.at[r, pl.ds(tile, SLAB), :]
        return copy(ref, ref, gg_s.at[o], gg_r.at[o], at_row(lax.rem(r + o, 4)))

    def offset_landed(o):
        ref = own_lg.at[lax.rem(r + 4 - o, 4), pl.ds(tile, SLAB), :]
        return copy(ref, ref, gg_s.at[o], gg_r.at[o], at_row(lax.rem(r + o, 4)))

    def swap(s, o):
        return copy(
            mid_out.at[s, o], mid_in.at[s, r, pl.ds(0, tile), :], swap_s.at[s, o], swap_r.at[s, o],
            at_row(lax.rem(r + o, 4)),
        )

    def swap_landed(s, o):
        return copy(
            mid_out.at[s, o], mid_in.at[s, lax.rem(r + 4 - o, 4), pl.ds(0, tile), :], swap_s.at[s, o],
            swap_r.at[s, o], at_row(lax.rem(r + o, 4)),
        )

    def composes(s):
        return k + 2**s < steps

    def makes_gain(s):
        return k + 2 ** (s + 1) < steps

    def sends_gain(s):
        return jnp.logical_and(k >= 2**s, k + 2**s < steps)

    def sends_spread(s):
        return k >= 2**s

    for n in range(4):
        cols = slice(n * tile, (n + 1) * tile)
        e_first[r, n] = e_in[0, :, cols]
    pl.semaphore_wait(barrier, len(partners))

    @pl.when(composes(0))
    def _():
        ring_start(0)

    @pl.when(sends_gain(0))
    def _():
        far_gain_piece(r).start()

    for n in range(4):
        cols = slice(n * tile, (n + 1) * tile)
        own_lg[n, pl.ds(0, tile), :] = l_in[0, :, cols]
    first_row = lax.broadcasted_iota(jnp.int32, (SLAB, tile), 0) == 0
    slab = jnp.broadcast_to(g_in[...].astype(F32), (SLAB, tile))
    own_lg[r, pl.ds(tile, SLAB), :] = jnp.where(first_row, slab, 0.0).astype(BF16)
    for o in (1, 2, 3):
        offset_piece(o).start()

    @pl.when(sends_spread(0))
    def _():
        far_spread(0).start()

    for o in (1, 2, 3):
        offset_landed(o).wait_recv()

    @pl.when(sends_spread(0))
    def _():
        far_offset().start()

    for s in range(levels):
        more = s + 1 < levels

        @pl.when(composes(s))
        def _():
            ring_relay(s)
            ring_near(s)
            if s == 0:

                @pl.when(sends_gain(0))
                def _():
                    far_gain_piece(left).start()
                    far_gain_piece(right).start()

                ring_opp(0)

                @pl.when(sends_gain(0))
                def _():
                    far_gain_piece(opp).start()

            elif more:

                @pl.when(makes_gain(s))
                def _():
                    far_gain(s).wait_recv()

                    @pl.loop(0, 4)
                    def _(a):
                        acc_e[a] = (
                            dot(gain(s, a, r), far_e[s, r])
                            + dot(gain(s, a, left), far_e[s, left])
                            + dot(gain(s, a, right), far_e[s, right])
                        )

                ring_opp(s)
            else:
                ring_opp(s)

            if more:

                @pl.when(makes_gain(s))
                def _():
                    if s == 0:
                        for b in range(4):
                            far_gain_piece(b).wait_recv()

                        @pl.loop(0, 4)
                        def _(a):
                            total = dot(gain(s, a, 0), far_e[s, 0])
                            for b in range(1, 4):
                                total += dot(gain(s, a, b), far_e[s, b])
                            e_later[s, r, a] = total.astype(BF16)
                    else:

                        @pl.loop(0, 4)
                        def _(a):
                            total = acc_e[a] + dot(gain(s, a, opp), far_e[s, opp])
                            e_later[s, r, a] = total.astype(BF16)

                    ring_start(s + 1)

                    @pl.when(sends_gain(s + 1))
                    def _():
                        far_gain(s + 1).start()

            far_spread(s).wait_recv()
            if s == 0:
                far_offset().wait_recv()
            for o in (2, 1, 3, 0):
                a = lax.rem(r + o, 4)
                total = dot_t(gain(s, a, 0), far_lg[s, 0, pl.ds(0, tile), :])
                for b in range(1, 4):
                    total += dot_t(gain(s, a, b), far_lg[s, b, pl.ds(0, tile), :])
                if o == 0:
                    mid_in[s, r, pl.ds(0, tile), :] = total.astype(BF16)
                else:
                    mid_out[s, o] = total.astype(BF16)
                    swap(s, o).start()
            for b in range(4):
                mid_in[s, b, pl.ds(tile, SLAB), :] = far_lg[s, b, pl.ds(tile, SLAB), :]
            for o in (1, 3, 2):
                swap_landed(s, o).wait_recv()

        @pl.when(sends_spread(s))
        def _():
            far_spread(s).wait_send()
            if s == 0:
                far_offset().wait_send()

        if s == 0:
            for o in (1, 2, 3):
                offset_piece(o).wait_send()

        @pl.when(composes(s))
        def _():
            @pl.loop(0, 4)
            def _(n):
                total = own_lg[n].astype(F32)
                for b in range(4):
                    total += dot_t(mid_in[s, b], gain(s, n, b))
                own_lg[n] = total.astype(BF16)

        if more:

            @pl.when(sends_spread(s + 1))
            def _():
                far_spread(s + 1).start()

    for n in range(4):
        cols = slice(n * tile, (n + 1) * tile)
        o_l[0, :, cols] = own_lg[n, pl.ds(0, tile), :]
    o_g[...] = own_lg[r, pl.ds(tile, SLAB), :][0:1]

    for s in range(levels):

        @pl.when(composes(s))
        def _():
            ring_sent(s)
            for o in (1, 2, 3):
                swap(s, o).wait_send()

        if s == 0:

            @pl.when(sends_gain(0))
            def _():
                for b in range(4):
                    far_gain_piece(b).wait_send()

        else:

            @pl.when(sends_gain(s))
            def _():
                far_gain(s).wait_send()


def per_device(gain_mats, offsets, spread_mats):
    steps = lax.axis_size("tm")
    levels = steps.bit_length() - 1
    tile = gain_mats.shape[1]
    dma = pltpu.SemaphoreType.DMA
    tall = tile + SLAB
    flops = levels * 3 * 2 * tile * (4 * tile) ** 2
    return pl.pallas_call(
        functools.partial(kernel, steps, levels, tile),
        name="scan",
        out_shape=(
            jax.ShapeDtypeStruct(offsets.shape, BF16),
            jax.ShapeDtypeStruct(spread_mats.shape, BF16),
        ),
        in_specs=[pl.BlockSpec(memory_space=pltpu.VMEM)] * 3,
        out_specs=[pl.BlockSpec(memory_space=pltpu.VMEM)] * 2,
        scratch_shapes=[
            pltpu.VMEM((4, 4, tile, tile), BF16),
            pltpu.VMEM((levels - 1, 4, 4, tile, tile), BF16),
            pltpu.VMEM((levels - 1, 4, tile, tile), BF16),
            pltpu.VMEM((levels, 4, tall, tile), BF16),
            pltpu.VMEM((levels, 4, tile, tile), BF16),
            pltpu.VMEM((levels, 4, tall, tile), BF16),
            pltpu.VMEM((4, tall, tile), BF16),
            pltpu.VMEM((4, tile, tile), F32),
            dma((levels, 2, 3)), dma((levels, 2, 3)),
            dma((levels, 4)), dma((levels, 4)),
            dma((levels, 4)), dma((levels, 4)),
            dma((levels,)), dma((levels,)),
            dma((4,)), dma((4,)),
            dma, dma,
        ],
        compiler_params=pltpu.CompilerParams(
            collective_id=0, has_side_effects=True, vmem_limit_bytes=48 * 2**20
        ),
        cost_estimate=pl.CostEstimate(flops=flops, bytes_accessed=3 * tile * 4 * tile * 2, transcendentals=0),
    )(gain_mats, offsets, spread_mats)


def solution(mesh):
    in_specs = (P("tm", "row", None), P("tm", "row"), P("tm", "row", None))
    out_specs = (P("tm", "row"), P("tm", "row", None))
    return jax.shard_map(per_device, mesh=mesh, in_specs=in_specs, out_specs=out_specs, check_vma=False)
```

```python
import functools

import jax
import jax.numpy as jnp
from jax import lax
from jax.experimental import pallas as pl
from jax.experimental.pallas import tpu as pltpu
from jax.sharding import PartitionSpec as P

MESH = pl.DeviceIdType.MESH
BF16 = jnp.bfloat16
F32 = jnp.float32
SLAB = 16


def dot(a, b):
    return jnp.dot(a, b, preferred_element_type=F32)


def dot_t(a, b):
    return lax.dot_general(a, b, (((1,), (1,)), ((), ())), preferred_element_type=F32)


def kernel(
    steps, levels, tile,
    e_in, g_in, l_in, o_g, o_l,
    e_first, e_later, far_e, far_lg, mid_out, mid_in, own_lg, acc_e, acc_m,
    ring_s, ring_r, swap_s, swap_r, fe_s, fe_r, fl_s, fl_r, gg_s, gg_r, fg_s, fg_r,
):
    k = lax.axis_index("tm")
    r = lax.axis_index("row")
    right, opp, left = (lax.rem(r + o, 4) for o in (1, 2, 3))

    def at_row(row):
        return (k, row)

    def at_step(step):
        return (step, r)

    def copy(src, dst, ssem, rsem, dev):
        return pltpu.make_async_remote_copy(
            src_ref=src, dst_ref=dst, send_sem=ssem, recv_sem=rsem, device_id=dev, device_id_type=MESH
        )

    barrier = pltpu.get_barrier_semaphore()
    partners = [at_row(right), at_row(opp), at_row(left)]
    for s in range(levels):
        partners.append(at_step(lax.rem(k + 2**s, steps)))
        if 2 ** (s + 1) != steps:
            partners.append(at_step(lax.rem(k + steps - 2**s, steps)))
    for dev in partners:
        pl.semaphore_signal(barrier, inc=1, device_id=dev, device_id_type=MESH)

    def blocks(s):
        return e_first if s == 0 else e_later.at[s - 1]

    def gain(s, a, b):
        return e_first[a, b] if s == 0 else e_later[s - 1, b, a]

    def ring(s, way, slot, blk, h):
        ref = blocks(s).at[blk, pl.ds(2 * h, 2)]
        dev = at_row(right if way == 0 else left)
        return copy(ref, ref, ring_s.at[s, way, slot], ring_r.at[s, way, slot], dev)

    def ring_start(s):
        ring(s, 0, 0, r, 0).start()
        ring(s, 1, 1, r, 1).start()
        ring(s, 0, 1, r, 1).start()
        ring(s, 1, 0, r, 0).start()

    def ring_relay(s):
        ring(s, 0, 0, left, 0).wait_recv()
        ring(s, 0, 2, left, 0).start()
        ring(s, 1, 1, right, 1).wait_recv()
        ring(s, 1, 2, right, 1).start()

    def ring_near(s):
        ring(s, 0, 1, left, 1).wait_recv()
        ring(s, 1, 0, right, 0).wait_recv()

    def ring_opp(s):
        ring(s, 0, 2, opp, 0).wait_recv()
        ring(s, 1, 2, opp, 1).wait_recv()

    def ring_sent(s):
        for way in range(2):
            ring(s, way, 0, r, 0).wait_send()
            ring(s, way, 1, r, 1).wait_send()
        ring(s, 0, 2, left, 0).wait_send()
        ring(s, 1, 2, right, 1).wait_send()

    def far_gain_piece(blk):
        return copy(e_first.at[blk, r], far_e.at[0, blk], fe_s.at[0, blk], fe_r.at[0, blk], at_step(k - 1))

    def far_gain(s):
        return copy(e_later.at[s - 1, r], far_e.at[s], fe_s.at[s, 0], fe_r.at[s, 0], at_step(k - 2**s))

    def far_spread(s, n):
        rows = pl.ds(0, tile if s == 0 else tile + SLAB)
        return copy(
            own_lg.at[n, rows, :], far_lg.at[s, n, rows, :], fl_s.at[s, n], fl_r.at[s, n], at_step(k - 2**s)
        )

    def far_offset():
        return copy(
            own_lg.at[:, pl.ds(tile, SLAB), :], far_lg.at[0, :, pl.ds(tile, SLAB), :], fg_s, fg_r, at_step(k - 1)
        )

    def offset_piece(o):
        ref = own_lg.at[r, pl.ds(tile, SLAB), :]
        return copy(ref, ref, gg_s.at[o], gg_r.at[o], at_row(lax.rem(r + o, 4)))

    def offset_landed(o):
        ref = own_lg.at[lax.rem(r + 4 - o, 4), pl.ds(tile, SLAB), :]
        return copy(ref, ref, gg_s.at[o], gg_r.at[o], at_row(lax.rem(r + o, 4)))

    def swap(s, o):
        return copy(
            mid_out.at[s, o], mid_in.at[s, r, pl.ds(0, tile), :], swap_s.at[s, o], swap_r.at[s, o],
            at_row(lax.rem(r + o, 4)),
        )

    def swap_landed(s, o):
        return copy(
            mid_out.at[s, o], mid_in.at[s, lax.rem(r + 4 - o, 4), pl.ds(0, tile), :], swap_s.at[s, o],
            swap_r.at[s, o], at_row(lax.rem(r + o, 4)),
        )

    def composes(s):
        return k + 2**s < steps

    def makes_gain(s):
        return k + 2 ** (s + 1) < steps

    def sends_gain(s):
        return jnp.logical_and(k >= 2**s, k + 2**s < steps)

    def sends_spread(s):
        return k >= 2**s

    for n in range(4):
        cols = slice(n * tile, (n + 1) * tile)
        e_first[r, n] = e_in[0, :, cols]
    pl.semaphore_wait(barrier, len(partners))

    @pl.when(composes(0))
    def _():
        ring_start(0)

    @pl.when(sends_gain(0))
    def _():
        far_gain_piece(r).start()

    for n in range(4):
        cols = slice(n * tile, (n + 1) * tile)
        own_lg[n, pl.ds(0, tile), :] = l_in[0, :, cols]
    first_row = lax.broadcasted_iota(jnp.int32, (SLAB, tile), 0) == 0
    slab = jnp.broadcast_to(g_in[...].astype(F32), (SLAB, tile))
    own_lg[r, pl.ds(tile, SLAB), :] = jnp.where(first_row, slab, 0.0).astype(BF16)
    for o in (1, 2, 3):
        offset_piece(o).start()

    @pl.when(sends_spread(0))
    def _():
        for n in range(4):
            far_spread(0, n).start()

    for o in (1, 2, 3):
        offset_landed(o).wait_recv()

    @pl.when(sends_spread(0))
    def _():
        far_offset().start()

    for s in range(levels):
        more = s + 1 < levels

        @pl.when(composes(s))
        def _():
            if s == 0:
                ring_relay(s)
            ring_near(s)
            if s == 0:

                @pl.when(sends_gain(0))
                def _():
                    far_gain_piece(left).start()
                    far_gain_piece(right).start()

                ring_opp(0)

                @pl.when(sends_gain(0))
                def _():
                    far_gain_piece(opp).start()

            elif more:

                @pl.when(makes_gain(s))
                def _():
                    far_gain(s).wait_recv()

                    for a in range(4):
                        acc_e[a] = (
                            dot(gain(s, a, r), far_e[s, r])
                            + dot(gain(s, a, left), far_e[s, left])
                            + dot(gain(s, a, right), far_e[s, right])
                        )

                ring_opp(s)
            else:
                ring_opp(s)

            if more:

                @pl.when(makes_gain(s))
                def _():
                    if s == 0:
                        for b in range(4):
                            far_gain_piece(b).wait_recv()

                        for a in range(4):
                            total = dot(gain(s, a, 0), far_e[s, 0])
                            for b in range(1, 4):
                                total += dot(gain(s, a, b), far_e[s, b])
                            e_later[s, r, a] = total.astype(BF16)
                    else:

                        for a in range(4):
                            total = acc_e[a] + dot(gain(s, a, opp), far_e[s, opp])
                            e_later[s, r, a] = total.astype(BF16)

                    ring_start(s + 1)

                    @pl.when(sends_gain(s + 1))
                    def _():
                        far_gain(s + 1).start()

            for b in range(4):
                far_spread(s, b).wait_recv()
                if b == 3:
                    break
                for o in range(4):
                    total = dot_t(gain(s, lax.rem(r + o, 4), b), far_lg[s, b, pl.ds(0, tile), :])
                    acc_m[o] = total if b == 0 else acc_m[o] + total
            if s == 0:
                far_offset().wait_recv()
            for o in (2, 1, 3, 0):
                a = lax.rem(r + o, 4)
                total = acc_m[o] + dot_t(gain(s, a, 3), far_lg[s, 3, pl.ds(0, tile), :])
                if o == 0:
                    mid_in[s, r, pl.ds(0, tile), :] = total.astype(BF16)
                else:
                    mid_out[s, o] = total.astype(BF16)
                    swap(s, o).start()
            for b in range(4):
                mid_in[s, b, pl.ds(tile, SLAB), :] = far_lg[s, b, pl.ds(tile, SLAB), :]
            if more:

                @pl.when(makes_gain(s))
                def _():
                    ring_relay(s + 1)

            for o in (1, 3, 2):
                swap_landed(s, o).wait_recv()

        @pl.when(sends_spread(s))
        def _():
            for n in range(4):
                far_spread(s, n).wait_send()
            if s == 0:
                far_offset().wait_send()

        if s == 0:
            for o in (1, 2, 3):
                offset_piece(o).wait_send()

        @pl.when(composes(s))
        def _():
            for n in range(4):
                total = own_lg[n].astype(F32)
                for b in range(4):
                    total += dot_t(mid_in[s, b], gain(s, n, b))
                own_lg[n] = total.astype(BF16)
                if more:

                    @pl.when(sends_spread(s + 1))
                    def _():
                        far_spread(s + 1, n).start()

        if more:

            @pl.when(jnp.logical_and(sends_spread(s + 1), jnp.logical_not(composes(s))))
            def _():
                for n in range(4):
                    far_spread(s + 1, n).start()

    for n in range(4):
        cols = slice(n * tile, (n + 1) * tile)
        o_l[0, :, cols] = own_lg[n, pl.ds(0, tile), :]
    o_g[...] = own_lg[r, pl.ds(tile, SLAB), :][0:1]

    for s in range(levels):

        @pl.when(composes(s))
        def _():
            ring_sent(s)
            for o in (1, 2, 3):
                swap(s, o).wait_send()

        if s == 0:

            @pl.when(sends_gain(0))
            def _():
                for b in range(4):
                    far_gain_piece(b).wait_send()

        else:

            @pl.when(sends_gain(s))
            def _():
                far_gain(s).wait_send()


def per_device(gain_mats, offsets, spread_mats):
    steps = lax.axis_size("tm")
    levels = steps.bit_length() - 1
    tile = gain_mats.shape[1]
    dma = pltpu.SemaphoreType.DMA
    tall = tile + SLAB
    flops = levels * 3 * 2 * tile * (4 * tile) ** 2
    return pl.pallas_call(
        functools.partial(kernel, steps, levels, tile),
        name="scan",
        out_shape=(
            jax.ShapeDtypeStruct(offsets.shape, BF16),
            jax.ShapeDtypeStruct(spread_mats.shape, BF16),
        ),
        in_specs=[pl.BlockSpec(memory_space=pltpu.VMEM)] * 3,
        out_specs=[pl.BlockSpec(memory_space=pltpu.VMEM)] * 2,
        scratch_shapes=[
            pltpu.VMEM((4, 4, tile, tile), BF16),
            pltpu.VMEM((levels - 1, 4, 4, tile, tile), BF16),
            pltpu.VMEM((levels - 1, 4, tile, tile), BF16),
            pltpu.VMEM((levels, 4, tall, tile), BF16),
            pltpu.VMEM((levels, 4, tile, tile), BF16),
            pltpu.VMEM((levels, 4, tall, tile), BF16),
            pltpu.VMEM((4, tall, tile), BF16),
            pltpu.VMEM((4, tile, tile), F32),
            pltpu.VMEM((4, tile, tile), F32),
            dma((levels, 2, 3)), dma((levels, 2, 3)),
            dma((levels, 4)), dma((levels, 4)),
            dma((levels, 4)), dma((levels, 4)),
            dma((levels, 4)), dma((levels, 4)),
            dma((4,)), dma((4,)),
            dma, dma,
        ],
        compiler_params=pltpu.CompilerParams(
            collective_id=0, has_side_effects=True, vmem_limit_bytes=48 * 2**20
        ),
        cost_estimate=pl.CostEstimate(flops=flops, bytes_accessed=3 * tile * 4 * tile * 2, transcendentals=0),
    )(gain_mats, offsets, spread_mats)


def solution(mesh):
    in_specs = (P("tm", "row", None), P("tm", "row"), P("tm", "row", None))
    out_specs = (P("tm", "row"), P("tm", "row", None))
    return jax.shard_map(per_device, mesh=mesh, in_specs=in_specs, out_specs=out_specs, check_vma=False)
```

```python
import functools

import jax
import jax.numpy as jnp
from jax import lax
from jax.experimental import pallas as pl
from jax.experimental.pallas import tpu as pltpu
from jax.sharding import PartitionSpec as P

MESH = pl.DeviceIdType.MESH
BF16 = jnp.bfloat16
F32 = jnp.float32
SLAB = 16


def dot(a, b):
    return jnp.dot(a, b, preferred_element_type=F32)


def dot_t(a, b):
    return lax.dot_general(a, b, (((1,), (1,)), ((), ())), preferred_element_type=F32)


def kernel(
    steps, levels, tile,
    e_in, g_in, l_in, o_g, o_l,
    stage_e, stage_l, stage_g, e_first, e_later, far_e, far_l, far_g, own_l, own_g, mid, acc_e, fin_l, fin_g,
    mve_s, mve_r, mvl_s, mvl_r, fed_s, fed_r, fe_s, fe_r, gd_s, gd_r, fgd_s, fgd_r, fg_s, fg_r,
    sib_s, sib_r, par_s, par_r, fwd_s, fwd_r,
    lf_s, lf_r, ls_s, ls_r, lp_s, lp_r, lw_s, lw_r, fin_s, fin_r, fing_s, fing_r,
):
    k = lax.axis_index("tm")
    y = lax.axis_index("row")
    core = k % 2
    column = k // 2
    parity = y // 2
    e = 2 * column + parity
    first = y + parity * (3 - 2 * y)
    q = first + core * (3 - 2 * first)
    q_sib = 3 - q
    q_par = q + 1 - 2 * (q % 2)
    q_dia = 3 - q_par
    sib = (k + 1 - 2 * core, y)
    par = (k, y + 1 - 2 * (y % 2))
    stays = parity == core
    moves = parity != core
    partner = (k + 1 - 2 * core, 3 - y)

    def holder(element, quarter):
        c = quarter // 2
        b = quarter + c * (3 - 2 * quarter)
        p = element % 2
        return (2 * (element // 2) + c, b + p * (3 - 2 * b))

    def copy(src, dst, ssem, rsem, dev):
        return pltpu.make_async_remote_copy(
            src_ref=src, dst_ref=dst, send_sem=ssem, recv_sem=rsem, device_id=dev, device_id_type=MESH
        )

    def composes(el, s):
        return el + 2**s < steps

    def makes_gain(el, s):
        return el + 2 ** (s + 1) < steps

    def sends_gain(el, s):
        return jnp.logical_and(el >= 2**s, el + 2**s < steps)

    def both(a, b):
        return jnp.logical_and(a, b)

    feeds_self = both(core == 1, y < 2)

    barrier = pltpu.get_barrier_semaphore()

    def greet(dev):
        pl.semaphore_signal(barrier, inc=1, device_id=dev, device_id_type=MESH)

    greet(sib)
    greet(par)
    for row in range(4):

        @pl.when(jnp.logical_not(both(stays, row == y)))
        def _():
            greet((e, row))

        @pl.when(both(e + 1 < steps, jnp.logical_not(both(feeds_self, row == y))))
        def _():
            greet((e + 1, row))

    for s in range(1, levels):

        @pl.when(composes(e, s))
        def _():
            greet((k + 2**s, y))

    def count(flag):
        return flag.astype(jnp.int32)

    greetings = 2 + 4 - count(stays) + count(k >= 1) * (4 - count(feeds_self))
    for s in range(1, levels):
        greetings += count(e >= 2**s)

    def blocks(s):
        return e_first if s == 0 else e_later.at[s - 1]

    def gain(s, a, b):
        return e_first[a, b] if s == 0 else e_later[s - 1, b, a]

    def half(s, blk, h):
        return blocks(s).at[blk, pl.ds(2 * h, 2)]

    def gain_sib(s, h):
        return copy(half(s, q, h), half(s, q, h), sib_s.at[s, h], sib_r.at[s, h], sib)

    def gain_sib_in(s, h):
        return copy(half(s, q_sib, h), half(s, q_sib, h), sib_s.at[s, h], sib_r.at[s, h], sib)

    def gain_par(s, h):
        return copy(half(s, q, h), half(s, q, h), par_s.at[s, h], par_r.at[s, h], par)

    def gain_par_in(s, h):
        return copy(half(s, q_par, h), half(s, q_par, h), par_s.at[s, h], par_r.at[s, h], par)

    def gain_fwd(s, h):
        return copy(half(s, q_par, h), half(s, q_par, h), fwd_s.at[s, h], fwd_r.at[s, h], sib)

    def gain_fwd_in(s, h):
        return copy(half(s, q_dia, h), half(s, q_dia, h), fwd_s.at[s, h], fwd_r.at[s, h], sib)

    def gain_start(s, h):
        gain_par(s, h).start()
        gain_sib(s, h).start()

    def far_gain(s):
        return copy(e_later.at[s - 1, q], far_e.at[s], fe_s.at[s], fe_r.at[s], (k - 2**s, y))

    def far_offset(s):
        return copy(own_g, far_g.at[s], fg_s.at[s], fg_r.at[s], (k - 2**s, y))

    def far_tile(s, t):
        return copy(own_l.at[(q + t) % 4], far_l.at[s, 3 * q + t], lf_s.at[s, t], lf_r.at[s, t], (k - 2**s, y))

    def tile_copy(s, t, owner, ssem, rsem, dev):
        ref = far_l.at[s, 3 * owner + t]
        return copy(ref, ref, ssem.at[s, t], rsem.at[s, t], dev)

    def tile_sib(s, t):
        return tile_copy(s, t, q, ls_s, ls_r, sib)

    def tile_sib_in(s, t):
        return tile_copy(s, t, q_sib, ls_s, ls_r, sib)

    def tile_par(s, t):
        return tile_copy(s, t, q, lp_s, lp_r, par)

    def tile_par_in(s, t):
        return tile_copy(s, t, q_par, lp_s, lp_r, par)

    def tile_fwd(s, t):
        return tile_copy(s, t, q_par, lw_s, lw_r, sib)

    def tile_fwd_in(s, t):
        return tile_copy(s, t, q_dia, lw_s, lw_r, sib)

    def if_tile(t, whose, run):
        if t < 2:
            run()
        else:
            pl.when(whose == 0)(run)

    def spread(s, a, b):
        t = (b - a) % 4
        if t < 2 or (t == 2 and a < 2):
            return far_l[s, 3 * a + t], False
        return far_l[s, 3 * b + (4 - t)], True

    def move_gain(h):
        return copy(stage_e.at[pl.ds(2 * h, 2)], e_first.at[y, pl.ds(2 * h, 2)], mve_s.at[h], mve_r.at[h], partner)

    def move_gain_in(h):
        return copy(stage_e.at[pl.ds(2 * h, 2)], e_first.at[q, pl.ds(2 * h, 2)], mve_s.at[h], mve_r.at[h], partner)

    def move_spread():
        return copy(stage_l, own_l, mvl_s, mvl_r, partner)

    def gain_direct(quarter):
        return copy(
            stage_e.at[quarter], far_e.at[0, y], fed_s.at[quarter], fed_r.at[y], holder(k - 1, quarter)
        )

    def gain_direct_in(row):
        return copy(stage_e.at[0], far_e.at[0, row], fed_s.at[row], fed_r.at[row], sib)

    def tile_direct(t):
        return copy(
            stage_l.at[(y + t) % 4], far_l.at[0, 3 * y + t], lf_s.at[0, t], lf_r.at[0, t], holder(k - 1, y)
        )

    def tile_in(s, t):
        return copy(own_l.at[0], far_l.at[s, 3 * q + t], lf_s.at[s, t], lf_r.at[s, t], sib)

    def offset_direct(quarter):
        return copy(stage_g, own_g.at[y], gd_s.at[quarter], gd_r.at[y], holder(k, quarter))

    def offset_direct_in(row):
        return copy(stage_g, own_g.at[row], gd_s.at[row], gd_r.at[row], sib)

    def offset_direct_far(quarter):
        return copy(stage_g, far_g.at[0, y], fgd_s.at[quarter], fgd_r.at[y], holder(k - 1, quarter))

    def offset_direct_far_in(row):
        return copy(stage_g, far_g.at[0, row], fgd_s.at[row], fgd_r.at[row], sib)

    def back(n):
        return copy(own_l.at[n], fin_l.at[n], fin_s.at[n], fin_r.at[n], partner)

    def back_offset():
        return copy(own_g.at[q], fin_g, fing_s, fing_r, partner)

    input_gain_sent = both(k >= 1, makes_gain(k - 1, 0))

    for n in range(4):
        stage_e[n] = e_in[0, :, n * tile : (n + 1) * tile]

    @pl.when(stays)
    def _():
        for n in range(4):
            e_first[q, n] = e_in[0, :, n * tile : (n + 1) * tile]

    pl.semaphore_wait(barrier, greetings)

    @pl.when(both(moves, composes(k, 0)))
    def _():
        move_gain(0).start()
        move_gain(1).start()

    @pl.when(both(stays, composes(e, 0)))
    def _():
        gain_start(0, 0)
        gain_start(0, 1)

    @pl.when(input_gain_sent)
    def _():
        for quarter in range(4):
            here = both(feeds_self, quarter == 3 - y)

            @pl.when(jnp.logical_not(here))
            def _():
                gain_direct(quarter).start()

            @pl.when(here)
            def _():
                far_e[0, y] = stage_e[quarter]

    for n in range(4):
        stage_l[n] = l_in[0, :, n * tile : (n + 1) * tile]
    first_row = lax.broadcasted_iota(jnp.int32, (SLAB, tile), 0) == 0
    slab = jnp.broadcast_to(g_in[...].astype(F32), (SLAB, tile))
    stage_g[...] = jnp.where(first_row, slab, 0.0).astype(BF16)

    @pl.when(k >= 1)
    def _():
        for t in range(3):
            if_tile(t, y // 2, lambda t=t: tile_direct(t).start())

    @pl.when(moves)
    def _():
        move_spread().start()

    for quarter in range(4):
        here = both(stays, quarter == y)

        @pl.when(jnp.logical_not(here))
        def _():
            offset_direct(quarter).start()

        @pl.when(here)
        def _():
            own_g[y] = stage_g[...]

    @pl.when(k >= 1)
    def _():
        for quarter in range(4):
            here = both(feeds_self, quarter == 3 - y)

            @pl.when(jnp.logical_not(here))
            def _():
                offset_direct_far(quarter).start()

            @pl.when(here)
            def _():
                far_g[0, y] = stage_g[...]

    @pl.when(stays)
    def _():
        for n in range(4):
            own_l[n] = l_in[0, :, n * tile : (n + 1) * tile]

    @pl.when(both(moves, composes(e, 0)))
    def _():
        move_gain_in(0).wait_recv()
        gain_start(0, 0)
        move_gain_in(1).wait_recv()
        gain_start(0, 1)

    for s in range(levels):
        more = s + 1 < levels

        def tiles_out():
            for t in range(3):

                def run(t=t):
                    tile_in(s, t).wait_recv()
                    tile_par(s, t).start()
                    tile_sib(s, t).start()

                if_tile(t, core, run)

        def tiles_on():
            for t in range(3):

                def run(t=t):
                    tile_par_in(s, t).wait_recv()
                    tile_fwd(s, t).start()

                if_tile(t, core, run)

        def tiles_rest():
            for t in range(3):

                def run(t=t):
                    tile_sib_in(s, t).wait_recv()
                    tile_fwd_in(s, t).wait_recv()

                if_tile(t, 1 - core, run)

        def gain_on(h):
            gain_par_in(s, h).wait_recv()
            gain_fwd(s, h).start()

        @pl.when(composes(e, s))
        def _():
            gain_on(0)
            tiles_out()
            gain_on(1)
            for h in range(2):
                gain_sib_in(s, h).wait_recv()

            if more:

                @pl.when(makes_gain(e, s))
                def _():
                    if s == 0:
                        for row in range(4):

                            @pl.when(jnp.logical_not(both(feeds_self, row == y)))
                            def _():
                                gain_direct_in(row).wait_recv()

                    else:
                        copy(far_e.at[s], far_e.at[s], fe_s.at[s], fe_r.at[s], sib).wait_recv()
                        for a in range(4):
                            acc_e[a] = (
                                dot(gain(s, a, q), far_e[s, q])
                                + dot(gain(s, a, q_sib), far_e[s, q_sib])
                                + dot(gain(s, a, q_par), far_e[s, q_par])
                            )

            for h in range(2):
                gain_fwd_in(s, h).wait_recv()

            if more:

                @pl.when(makes_gain(e, s))
                def _():
                    for h in range(2):
                        for a in (2 * h, 2 * h + 1):
                            if s == 0:
                                total = dot(gain(s, a, 0), far_e[s, 0])
                                for b in range(1, 4):
                                    total += dot(gain(s, a, b), far_e[s, b])
                            else:
                                total = acc_e[a] + dot(gain(s, a, q_dia), far_e[s, q_dia])
                            e_later[s, q, a] = total.astype(BF16)
                        gain_start(s + 1, h)

                    @pl.when(sends_gain(e, s + 1))
                    def _():
                        far_gain(s + 1).start()

            tiles_on()
            tiles_rest()
            for n in range(4):
                total = None
                for b in range(4):
                    part, turned = spread(s, b, n)
                    term = (dot_t if turned else dot)(gain(s, q, b), part)
                    total = term if total is None else total + term
                mid[n, pl.ds(0, tile), :] = total.astype(BF16)
            if s == 0:
                for row in range(4):

                    @pl.when(jnp.logical_not(both(feeds_self, row == y)))
                    def _():
                        offset_direct_far_in(row).wait_recv()

            else:
                copy(far_g.at[s], far_g.at[s], fg_s.at[s], fg_r.at[s], sib).wait_recv()
            for b in range(4):
                mid[b, pl.ds(tile, SLAB), :] = far_g[s, b]

        if s == 0:

            @pl.when(moves)
            def _():
                move_spread().wait_recv()

            for row in range(4):

                @pl.when(jnp.logical_not(both(stays, row == y)))
                def _():
                    offset_direct_in(row).wait_recv()

        else:

            @pl.when(e >= 2**s)
            def _():
                for t in range(3):
                    if_tile(t, core, lambda t=t: far_tile(s, t).wait_send())
                far_offset(s).wait_send()

        @pl.when(composes(e, s))
        def _():
            for o in range(4):
                n = (q + o) % 4
                total = dot_t(mid[0], gain(s, n, 0))
                for b in range(1, 4):
                    total += dot_t(mid[b], gain(s, n, b))
                own_l[n] = (total[0:tile] + own_l[n].astype(F32)).astype(BF16)
                own_g[n] = (total[tile:] + own_g[n].astype(F32)).astype(BF16)
                if more:
                    if o < 3:

                        @pl.when(e >= 2 ** (s + 1))
                        def _():
                            if_tile(o, core, lambda: far_tile(s + 1, o).start())

                else:

                    @pl.when(moves)
                    def _():
                        back(n).start()

        if more:

            @pl.when(both(e >= 2 ** (s + 1), jnp.logical_not(composes(e, s))))
            def _():
                for t in range(3):
                    if_tile(t, core, lambda t=t: far_tile(s + 1, t).start())

            @pl.when(e >= 2 ** (s + 1))
            def _():
                far_offset(s + 1).start()

        else:

            @pl.when(both(moves, jnp.logical_not(composes(e, s))))
            def _():
                for n in range(4):
                    back(n).start()

    @pl.when(moves)
    def _():
        back_offset().start()
        for o in range(4):
            n = (y + o) % 4
            copy(own_l.at[n], fin_l.at[n], fin_s.at[n], fin_r.at[n], partner).wait_recv()
        for n in range(4):
            o_l[0, :, n * tile : (n + 1) * tile] = fin_l[n]
        back_offset().wait_recv()
        o_g[...] = fin_g[0:1]

    @pl.when(stays)
    def _():
        for n in range(4):
            o_l[0, :, n * tile : (n + 1) * tile] = own_l[n]
        o_g[...] = own_g[q][0:1]

    @pl.when(moves)
    def _():
        back_offset().wait_send()
        for n in range(4):
            back(n).wait_send()
        move_spread().wait_send()

    @pl.when(both(moves, composes(k, 0)))
    def _():
        move_gain(0).wait_send()
        move_gain(1).wait_send()

    for quarter in range(4):
        here = both(feeds_self, quarter == 3 - y)

        @pl.when(both(input_gain_sent, jnp.logical_not(here)))
        def _():
            gain_direct(quarter).wait_send()

        @pl.when(both(k >= 1, jnp.logical_not(here)))
        def _():
            offset_direct_far(quarter).wait_send()

        @pl.when(jnp.logical_not(both(stays, quarter == y)))
        def _():
            offset_direct(quarter).wait_send()

    @pl.when(k >= 1)
    def _():
        for t in range(3):
            if_tile(t, y // 2, lambda t=t: tile_direct(t).wait_send())

    for s in range(levels):

        @pl.when(composes(e, s))
        def _():
            for h in range(2):
                gain_par(s, h).wait_send()
                gain_sib(s, h).wait_send()
                gain_fwd(s, h).wait_send()
            for t in range(3):

                def run(t=t):
                    tile_par(s, t).wait_send()
                    tile_sib(s, t).wait_send()
                    tile_fwd(s, t).wait_send()

                if_tile(t, core, run)

        if s > 0:

            @pl.when(sends_gain(e, s))
            def _():
                far_gain(s).wait_send()


def per_device(gain_mats, offsets, spread_mats):
    steps = lax.axis_size("tm")
    levels = steps.bit_length() - 1
    tile = gain_mats.shape[1]
    dma = pltpu.SemaphoreType.DMA
    flops = levels * 3 * 2 * tile * (4 * tile) ** 2
    square = (tile, tile)
    return pl.pallas_call(
        functools.partial(kernel, steps, levels, tile),
        name="scan",
        out_shape=(
            jax.ShapeDtypeStruct(offsets.shape, BF16),
            jax.ShapeDtypeStruct(spread_mats.shape, BF16),
        ),
        in_specs=[pl.BlockSpec(memory_space=pltpu.VMEM)] * 3,
        out_specs=[pl.BlockSpec(memory_space=pltpu.VMEM)] * 2,
        scratch_shapes=[
            pltpu.VMEM((4, *square), BF16),
            pltpu.VMEM((4, *square), BF16),
            pltpu.VMEM((SLAB, tile), BF16),
            pltpu.VMEM((4, 4, *square), BF16),
            pltpu.VMEM((levels - 1, 4, 4, *square), BF16),
            pltpu.VMEM((levels - 1, 4, *square), BF16),
            pltpu.VMEM((levels, 12, *square), BF16),
            pltpu.VMEM((levels, 4, SLAB, tile), BF16),
            pltpu.VMEM((4, *square), BF16),
            pltpu.VMEM((4, SLAB, tile), BF16),
            pltpu.VMEM((4, tile + SLAB, tile), BF16),
            pltpu.VMEM((4, *square), F32),
            pltpu.VMEM((4, *square), BF16),
            pltpu.VMEM((SLAB, tile), BF16),
            dma((2,)), dma((2,)), dma, dma,
            dma((4,)), dma((4,)), dma((levels,)), dma((levels,)),
            dma((4,)), dma((4,)), dma((4,)), dma((4,)), dma((levels,)), dma((levels,)),
            dma((levels, 2)), dma((levels, 2)), dma((levels, 2)), dma((levels, 2)), dma((levels, 2)), dma((levels, 2)),
            dma((levels, 3)), dma((levels, 3)), dma((levels, 3)), dma((levels, 3)),
            dma((levels, 3)), dma((levels, 3)), dma((levels, 3)), dma((levels, 3)),
            dma((4,)), dma((4,)), dma, dma,
        ],
        compiler_params=pltpu.CompilerParams(
            collective_id=0, has_side_effects=True, vmem_limit_bytes=48 * 2**20
        ),
        cost_estimate=pl.CostEstimate(flops=flops, bytes_accessed=3 * tile * 4 * tile * 2, transcendentals=0),
    )(gain_mats, offsets, spread_mats)


def solution(mesh):
    in_specs = (P("tm", "row", None), P("tm", "row"), P("tm", "row", None))
    out_specs = (P("tm", "row"), P("tm", "row", None))
    return jax.shard_map(per_device, mesh=mesh, in_specs=in_specs, out_specs=out_specs, check_vma=False)
```

```python
import functools

import jax
import jax.numpy as jnp
from jax import lax
from jax.experimental import pallas as pl
from jax.experimental.pallas import tpu as pltpu
from jax.sharding import PartitionSpec as P

MESH = pl.DeviceIdType.MESH
BF16 = jnp.bfloat16
F32 = jnp.float32
PLAN = (
    "D0", "T0", "P0", "O0", "B00", "B01", "g00", "t00", "t01", "g01", "b0", "n0", "w0", "E0", "F10", "F11", "F12", "F13", "H1", "t02",
    "t03", "t04", "t05", "G10", "G11", "u00", "u01", "u02", "u03", "u04", "u05", "M0", "L0", "g10", "t10", "t11", "g11", "b1", "n1", "w1",
    "E1", "F20", "F21", "F22", "F23", "H2", "t12", "t13", "t14", "t15", "G20", "G21", "u10", "u11", "u12", "u13", "u14", "u15", "M1", "L1",
    "g20", "t20", "t21", "g21", "b2", "n2", "w2", "E2", "F30", "F31", "F32", "F33", "H3", "t22", "t23", "t24", "t25", "G30", "G31", "u20",
    "u21", "u22", "u23", "u24", "u25", "M2", "L2", "g30", "t30", "t31", "g31", "b3", "n3", "w3", "E3", "F40", "F41", "F42", "F43", "H4",
    "t32", "t33", "t34", "t35", "G40", "G41", "u30", "u31", "u32", "u33", "u34", "u35", "M3", "L3", "g40", "t40", "t41", "g41", "b4", "w4",
    "t42", "t43", "t44", "t45", "u40", "u41", "u42", "u43", "u44", "u45", "M4", "L4",
)
HALVES = 2
FARS = 4
PARTS = 2
SLAB = 16


def dot(a, b):
    return jnp.dot(a, b, preferred_element_type=F32)


def dot_t(a, b):
    return lax.dot_general(a, b, (((1,), (1,)), ((), ())), preferred_element_type=F32)


def kernel(
    steps, levels, tile,
    e_in, g_in, l_in, o_g, o_l,
    stage_e, stage_l, stage_g, e_first, e_later, far_e, far_l, far_g, own_l, own_g, mid, acc_e, fin_l, fin_g, offset_row,
    mve_s, mve_r, mvl_s, mvl_r, fed_s, fed_r, fe_s, fe_r, gd_s, gd_r, fgd_s, fgd_r, fg_s, fg_r,
    sib_s, sib_r, par_s, par_r, fwd_s, fwd_r,
    lf_s, lf_r, ls_s, ls_r, lp_s, lp_r, lw_s, lw_r, fin_s, fin_r, fing_s, fing_r, in_s, out_s, off_s,
):
    k = lax.axis_index("tm")
    y = lax.axis_index("row")
    core = k % 2
    column = k // 2
    parity = y // 2
    e = 2 * column + parity
    first = y + parity * (3 - 2 * y)
    q = first + core * (3 - 2 * first)
    q_sib = 3 - q
    q_par = q + 1 - 2 * (q % 2)
    q_dia = 3 - q_par
    sib = (k + 1 - 2 * core, y)
    par = (k, y + 1 - 2 * (y % 2))
    stays = parity == core
    moves = parity != core
    partner = (k + 1 - 2 * core, 3 - y)

    def holder(element, quarter):
        c = quarter // 2
        b = quarter + c * (3 - 2 * quarter)
        p = element % 2
        return (2 * (element // 2) + c, b + p * (3 - 2 * b))

    def copy(src, dst, ssem, rsem, dev):
        return pltpu.make_async_remote_copy(
            src_ref=src, dst_ref=dst, send_sem=ssem, recv_sem=rsem, device_id=dev, device_id_type=MESH
        )

    def composes(el, s):
        return el + 2**s < steps

    def makes_gain(el, s):
        return el + 2 ** (s + 1) < steps

    def sends_gain(el, s):
        return jnp.logical_and(el >= 2**s, el + 2**s < steps)

    def both(a, b):
        return jnp.logical_and(a, b)

    feeds_self = both(core == 1, y < 2)

    barrier = pltpu.get_barrier_semaphore()

    def greet(dev):
        pl.semaphore_signal(barrier, inc=1, device_id=dev, device_id_type=MESH)

    greet(sib)
    greet(par)
    for row in range(4):

        @pl.when(jnp.logical_not(both(stays, row == y)))
        def _():
            greet((e, row))

        @pl.when(both(e + 1 < steps, jnp.logical_not(both(feeds_self, row == y))))
        def _():
            greet((e + 1, row))

    for s in range(1, levels):

        @pl.when(composes(e, s))
        def _():
            greet((k + 2**s, y))

    def count(flag):
        return flag.astype(jnp.int32)

    greetings = 2 + 4 - count(stays) + count(k >= 1) * (4 - count(feeds_self))
    for s in range(1, levels):
        greetings += count(e >= 2**s)

    def blocks(s):
        return e_first if s == 0 else e_later.at[s - 1]

    def gain(s, a, b):
        return e_first[a, b] if s == 0 else e_later[s - 1, b, a]

    parts = PARTS
    tiles = 4 // parts

    def half(s, blk, h):
        return blocks(s).at[blk, pl.ds(tiles * h, tiles)]

    def gain_sib(s, h):
        return copy(half(s, q, h), half(s, q, h), sib_s.at[s, h], sib_r.at[s, h], sib)

    def gain_sib_in(s, h):
        return copy(half(s, q_sib, h), half(s, q_sib, h), sib_s.at[s, h], sib_r.at[s, h], sib)

    def gain_par(s, h):
        return copy(half(s, q, h), half(s, q, h), par_s.at[s, h], par_r.at[s, h], par)

    def gain_par_in(s, h):
        return copy(half(s, q_par, h), half(s, q_par, h), par_s.at[s, h], par_r.at[s, h], par)

    def gain_fwd(s, h):
        return copy(half(s, q_par, h), half(s, q_par, h), fwd_s.at[s, h], fwd_r.at[s, h], sib)

    def gain_fwd_in(s, h):
        return copy(half(s, q_dia, h), half(s, q_dia, h), fwd_s.at[s, h], fwd_r.at[s, h], sib)

    def gain_start(s, h):
        gain_par(s, h).start()

    def far_gain(s, h):
        part = pl.ds(h * (4 // FARS), 4 // FARS)
        return copy(e_later.at[s - 1, q, part], far_e.at[s, part], fe_s.at[s, h], fe_r.at[s, h], (k - 2**s, y))

    def far_offset(s):
        return copy(own_g, far_g.at[s], fg_s.at[s], fg_r.at[s], (k - 2**s, y))

    pieces = 3 * HALVES

    def rows(c):
        return pl.ds(c % HALVES * (tile // HALVES), tile // HALVES)

    def far_tile(s, c):
        t = c // HALVES
        return copy(
            own_l.at[(q + t) % 4, rows(c)], far_l.at[s, 3 * q + t, rows(c)], lf_s.at[s, c], lf_r.at[s, c], (k - 2**s, y)
        )

    def tile_copy(s, c, owner, ssem, rsem, dev):
        ref = far_l.at[s, 3 * owner + c // HALVES, rows(c)]
        return copy(ref, ref, ssem.at[s, c], rsem.at[s, c], dev)

    def tile_sib(s, t):
        return tile_copy(s, t, q, ls_s, ls_r, sib)

    def tile_sib_in(s, t):
        return tile_copy(s, t, q_sib, ls_s, ls_r, sib)

    def tile_par(s, t):
        return tile_copy(s, t, q, lp_s, lp_r, par)

    def tile_par_in(s, t):
        return tile_copy(s, t, q_par, lp_s, lp_r, par)

    def tile_fwd(s, t):
        return tile_copy(s, t, q_par, lw_s, lw_r, sib)

    def tile_fwd_in(s, t):
        return tile_copy(s, t, q_dia, lw_s, lw_r, sib)

    def if_tile(t, whose, run):
        if t < 2 * HALVES:
            run()
        else:
            pl.when(whose == 0)(run)

    def spread(s, a, b):
        t = (b - a) % 4
        if t < 2 or (t == 2 and a < 2):
            return far_l[s, 3 * a + t], False
        return far_l[s, 3 * b + (4 - t)], True

    def move_gain(h):
        part = pl.ds(tiles * h, tiles)
        return copy(stage_e.at[part], e_first.at[y, part], mve_s.at[h], mve_r.at[h], partner)

    def move_gain_in(h):
        part = pl.ds(tiles * h, tiles)
        return copy(stage_e.at[part], e_first.at[q, part], mve_s.at[h], mve_r.at[h], partner)

    def move_spread():
        return copy(stage_l, own_l, mvl_s, mvl_r, partner)

    def gain_direct(quarter):
        return copy(
            stage_e.at[quarter], far_e.at[0, y], fed_s.at[quarter], fed_r.at[y], holder(k - 1, quarter)
        )

    def gain_direct_in(row):
        return copy(stage_e.at[0], far_e.at[0, row], fed_s.at[row], fed_r.at[row], sib)

    def tile_direct(c):
        t = c // HALVES
        return copy(
            stage_l.at[(y + t) % 4, rows(c)], far_l.at[0, 3 * y + t, rows(c)], lf_s.at[0, c], lf_r.at[0, c],
            holder(k - 1, y),
        )

    def tile_in(s, c):
        return copy(own_l.at[0, rows(c)], far_l.at[s, 3 * q + c // HALVES, rows(c)], lf_s.at[s, c], lf_r.at[s, c], sib)

    def offset_direct(quarter):
        return copy(stage_g, own_g.at[y], gd_s.at[quarter], gd_r.at[y], holder(k, quarter))

    def offset_direct_in(row):
        return copy(stage_g, own_g.at[row], gd_s.at[row], gd_r.at[row], sib)

    def offset_direct_far(quarter):
        return copy(stage_g, far_g.at[0, y], fgd_s.at[quarter], fgd_r.at[y], holder(k - 1, quarter))

    def offset_direct_far_in(row):
        return copy(stage_g, far_g.at[0, row], fgd_s.at[row], fgd_r.at[row], sib)

    def load_gain(n):
        return pltpu.make_async_copy(e_in.at[0, :, pl.ds(n * tile, tile)], stage_e.at[n], in_s.at[0, n])

    def load_own_gain(n):
        return pltpu.make_async_copy(e_in.at[0, :, pl.ds(n * tile, tile)], e_first.at[q, n], in_s.at[1, n])

    def load_spread(n):
        return pltpu.make_async_copy(l_in.at[0, :, pl.ds(n * tile, tile)], stage_l.at[n], in_s.at[2, n])

    def load_own_spread(n):
        return pltpu.make_async_copy(l_in.at[0, :, pl.ds(n * tile, tile)], own_l.at[n], in_s.at[3, n])

    def store_own(n):
        return pltpu.make_async_copy(own_l.at[n], o_l.at[0, :, pl.ds(pl.multiple_of(n * tile, tile), tile)], out_s.at[n])

    def store_back(n):
        return pltpu.make_async_copy(fin_l.at[n], o_l.at[0, :, pl.ds(pl.multiple_of(n * tile, tile), tile)], out_s.at[n])

    def back(n):
        return copy(own_l.at[n], fin_l.at[n], fin_s.at[n], fin_r.at[n], partner)

    def back_offset():
        return copy(own_g.at[q], fin_g, fing_s, fing_r, partner)

    input_gain_sent = both(k >= 1, makes_gain(k - 1, 0))

    for n in range(4):
        load_spread(n).start()
    for n in range(4):
        load_gain(n).start()

    @pl.when(stays)
    def _():
        for n in range(4):
            load_own_gain(n).start()
        for n in range(4):
            load_own_spread(n).start()

    load_offset = pltpu.make_async_copy(g_in, offset_row, off_s)
    load_offset.start()
    load_offset.wait()
    first_row = lax.broadcasted_iota(jnp.int32, (SLAB, tile), 0) == 0
    slab = jnp.broadcast_to(offset_row[...].astype(F32), (SLAB, tile))
    stage_g[...] = jnp.where(first_row, slab, 0.0).astype(BF16)
    for n in range(4):
        load_spread(n).wait()
    for n in range(4):
        load_gain(n).wait()

    @pl.when(stays)
    def _():
        for n in range(4):
            load_own_gain(n).wait()

    pl.semaphore_wait(barrier, greetings)

    @pl.when(both(moves, composes(k, 0)))
    def _():
        for h in range(parts):
            move_gain(h).start()

    @pl.when(both(stays, composes(e, 0)))
    def _():
        for h in range(parts):
            gain_start(0, h)
        for h in range(parts):
            gain_sib(0, h).start()

    @pl.when(stays)
    def _():
        for n in range(4):
            load_own_spread(n).wait()

    def ring_moved(s, h):
        @pl.when(both(moves, composes(e, s)))
        def _():
            move_gain_in(h).wait_recv()
            gain_start(s, h)
            gain_sib(s, h).start()

    def tiles_direct(s):
        @pl.when(k >= 1)
        def _():
            for c in range(pieces):
                if_tile(c, y // 2, lambda c=c: tile_direct(c).start())

    def offsets_out(s):
        for quarter in range(4):
            here = both(stays, quarter == y)

            @pl.when(jnp.logical_not(here))
            def _():
                offset_direct(quarter).start()

            @pl.when(here)
            def _():
                own_g[y] = stage_g[...]

        @pl.when(k >= 1)
        def _():
            for quarter in range(4):
                here = both(feeds_self, quarter == 3 - y)

                @pl.when(jnp.logical_not(here))
                def _():
                    offset_direct_far(quarter).start()

                @pl.when(here)
                def _():
                    far_g[0, y] = stage_g[...]

    def spread_out(s):
        @pl.when(moves)
        def _():
            move_spread().start()

    def direct_out(s):
        @pl.when(input_gain_sent)
        def _():
            for quarter in range(4):
                here = both(feeds_self, quarter == 3 - y)

                @pl.when(jnp.logical_not(here))
                def _():
                    gain_direct(quarter).start()

                @pl.when(here)
                def _():
                    far_e[0, y] = stage_e[quarter]

    def ring_out(s, h):
        @pl.when(composes(e, s))
        def _():
            gain_start(s, h)

    def ring_near(s):
        @pl.when(composes(e, s))
        def _():
            for h in range(parts):
                gain_sib(s, h).start()

    def far_out(s, h):
        @pl.when(sends_gain(e, s))
        def _():
            far_gain(s, h).start()

    def ring_on(s, h):
        @pl.when(composes(e, s))
        def _():
            gain_par_in(s, h).wait_recv()
            gain_fwd(s, h).start()

    def tile_on(s, t):
        def run():
            tile_in(s, t).wait_recv()
            tile_par(s, t).start()
            tile_sib(s, t).start()

        @pl.when(composes(e, s))
        def _():
            if_tile(t, core, run)

    def tile_over(s, t):
        def run():
            tile_par_in(s, t).wait_recv()
            tile_fwd(s, t).start()

        @pl.when(composes(e, s))
        def _():
            if_tile(t, core, run)

    def gain_beside(s):
        @pl.when(composes(e, s))
        def _():
            for h in range(parts):
                gain_sib_in(s, h).wait_recv()

    def gain_near(s):
        @pl.when(makes_gain(e, s))
        def _():
            if s == 0:
                for row in range(4):

                    @pl.when(jnp.logical_not(both(feeds_self, row == y)))
                    def _():
                        gain_direct_in(row).wait_recv()

            else:
                for h in range(FARS):
                    far_gain(s, h).wait_recv()
                for a in range(4):
                    acc_e[a] = (
                        dot(gain(s, a, q), far_e[s, q])
                        + dot(gain(s, a, q_sib), far_e[s, q_sib])
                        + dot(gain(s, a, q_par), far_e[s, q_par])
                    )

    def gain_whole(s):
        @pl.when(composes(e, s))
        def _():
            for h in range(parts):
                gain_fwd_in(s, h).wait_recv()

    def gain_new(s):
        @pl.when(makes_gain(e, s))
        def _():
            for a in range(4):
                if s == 0:
                    total = dot(gain(s, a, 0), far_e[s, 0])
                    for b in range(1, 4):
                        total += dot(gain(s, a, b), far_e[s, b])
                else:
                    total = acc_e[a] + dot(gain(s, a, q_dia), far_e[s, q_dia])
                e_later[s, q, a] = total.astype(BF16)

    def middle(s):
        @pl.when(composes(e, s))
        def _():
            for t in range(pieces):

                def run(t=t):
                    tile_sib_in(s, t).wait_recv()
                    tile_fwd_in(s, t).wait_recv()

                if_tile(t, 1 - core, run)
            for n in range(4):
                total = None
                for b in range(4):
                    part, turned = spread(s, b, n)
                    term = (dot_t if turned else dot)(gain(s, q, b), part)
                    total = term if total is None else total + term
                mid[n, pl.ds(0, tile), :] = total.astype(BF16)
            if s == 0:
                for row in range(4):

                    @pl.when(jnp.logical_not(both(feeds_self, row == y)))
                    def _():
                        offset_direct_far_in(row).wait_recv()

            else:
                copy(far_g.at[s], far_g.at[s], fg_s.at[s], fg_r.at[s], sib).wait_recv()
            for b in range(4):
                mid[b, pl.ds(tile, SLAB), :] = far_g[s, b]

    def spread_new(s):
        more = s + 1 < levels
        if s == 0:

            @pl.when(moves)
            def _():
                move_spread().wait_recv()

            for row in range(4):

                @pl.when(jnp.logical_not(both(stays, row == y)))
                def _():
                    offset_direct_in(row).wait_recv()

        else:

            @pl.when(e >= 2**s)
            def _():
                for t in range(pieces):
                    if_tile(t, core, lambda t=t: far_tile(s, t).wait_send())
                far_offset(s).wait_send()

        @pl.when(composes(e, s))
        def _():
            for o in range(4):
                n = (q + o) % 4
                total = dot_t(mid[0], gain(s, n, 0))
                for b in range(1, 4):
                    total += dot_t(mid[b], gain(s, n, b))
                own_l[n] = (total[0:tile] + own_l[n].astype(F32)).astype(BF16)
                own_g[n] = (total[tile:] + own_g[n].astype(F32)).astype(BF16)
                if more:
                    if o < 3:

                        @pl.when(e >= 2 ** (s + 1))
                        def _():
                            for c in range(HALVES * o, HALVES * (o + 1)):
                                if_tile(c, core, lambda c=c: far_tile(s + 1, c).start())

                else:

                    @pl.when(moves)
                    def _():
                        back(n).start()

                    @pl.when(stays)
                    def _():
                        store_own(n).start()

        if more:

            @pl.when(both(e >= 2 ** (s + 1), jnp.logical_not(composes(e, s))))
            def _():
                for t in range(pieces):
                    if_tile(t, core, lambda t=t: far_tile(s + 1, t).start())

            @pl.when(e >= 2 ** (s + 1))
            def _():
                far_offset(s + 1).start()

        else:

            @pl.when(both(moves, jnp.logical_not(composes(e, s))))
            def _():
                for n in range(4):
                    back(n).start()

            @pl.when(both(stays, jnp.logical_not(composes(e, s))))
            def _():
                for n in range(4):
                    store_own(n).start()

    steps_of = dict(
        B=ring_moved, D=direct_out, T=tiles_direct, P=spread_out, O=offsets_out, b=gain_beside, G=ring_out, H=ring_near, F=far_out, g=ring_on, t=tile_on, u=tile_over, n=gain_near, w=gain_whole, E=gain_new, M=middle,
        L=spread_new,
    )
    for word in PLAN:
        args = [int(digit) for digit in word[1:]]
        steps_of[word[0]](*args)

    @pl.when(moves)
    def _():
        back_offset().start()
        for o in range(4):
            n = (y + o) % 4
            copy(own_l.at[n], fin_l.at[n], fin_s.at[n], fin_r.at[n], partner).wait_recv()
            store_back(n).start()
        back_offset().wait_recv()
        o_g[...] = fin_g[0:1]

    @pl.when(stays)
    def _():
        o_g[...] = own_g[q][0:1]

    for n in range(4):
        store_own(n).wait()
    @pl.when(moves)
    def _():
        back_offset().wait_send()
        for n in range(4):
            back(n).wait_send()
        move_spread().wait_send()

    @pl.when(both(moves, composes(k, 0)))
    def _():
        for h in range(parts):
            move_gain(h).wait_send()

    for quarter in range(4):
        here = both(feeds_self, quarter == 3 - y)

        @pl.when(both(input_gain_sent, jnp.logical_not(here)))
        def _():
            gain_direct(quarter).wait_send()

        @pl.when(both(k >= 1, jnp.logical_not(here)))
        def _():
            offset_direct_far(quarter).wait_send()

        @pl.when(jnp.logical_not(both(stays, quarter == y)))
        def _():
            offset_direct(quarter).wait_send()

    @pl.when(k >= 1)
    def _():
        for t in range(pieces):
            if_tile(t, y // 2, lambda t=t: tile_direct(t).wait_send())

    for s in range(levels):

        @pl.when(composes(e, s))
        def _():
            for h in range(parts):
                gain_par(s, h).wait_send()
                gain_sib(s, h).wait_send()
                gain_fwd(s, h).wait_send()
            for t in range(pieces):

                def run(t=t):
                    tile_par(s, t).wait_send()
                    tile_sib(s, t).wait_send()
                    tile_fwd(s, t).wait_send()

                if_tile(t, core, run)

        if s > 0:

            @pl.when(sends_gain(e, s))
            def _():
                for h in range(FARS):
                    far_gain(s, h).wait_send()


def per_device(gain_mats, offsets, spread_mats):
    steps = lax.axis_size("tm")
    levels = steps.bit_length() - 1
    tile = gain_mats.shape[1]
    dma = pltpu.SemaphoreType.DMA
    flops = levels * 3 * 2 * tile * (4 * tile) ** 2
    square = (tile, tile)
    return pl.pallas_call(
        functools.partial(kernel, steps, levels, tile),
        name="scan",
        out_shape=(
            jax.ShapeDtypeStruct(offsets.shape, BF16),
            jax.ShapeDtypeStruct(spread_mats.shape, BF16),
        ),
        in_specs=[pl.BlockSpec(memory_space=pltpu.HBM)] * 3,
        out_specs=[pl.BlockSpec(memory_space=pltpu.VMEM)] * 2,
        scratch_shapes=[
            pltpu.VMEM((4, *square), BF16),
            pltpu.VMEM((4, *square), BF16),
            pltpu.VMEM((SLAB, tile), BF16),
            pltpu.VMEM((4, 4, *square), BF16),
            pltpu.VMEM((levels - 1, 4, 4, *square), BF16),
            pltpu.VMEM((levels - 1, 4, *square), BF16),
            pltpu.VMEM((levels, 12, *square), BF16),
            pltpu.VMEM((levels, 4, SLAB, tile), BF16),
            pltpu.VMEM((4, *square), BF16),
            pltpu.VMEM((4, SLAB, tile), BF16),
            pltpu.VMEM((4, tile + SLAB, tile), BF16),
            pltpu.VMEM((4, *square), F32),
            pltpu.VMEM((4, *square), BF16),
            pltpu.VMEM((SLAB, tile), BF16),
            pltpu.VMEM((1, tile), BF16),
            dma((4,)), dma((4,)), dma, dma,
            dma((4,)), dma((4,)), dma((levels, 4)), dma((levels, 4)),
            dma((4,)), dma((4,)), dma((4,)), dma((4,)), dma((levels,)), dma((levels,)),
            dma((levels, 4)), dma((levels, 4)), dma((levels, 4)), dma((levels, 4)), dma((levels, 4)), dma((levels, 4)),
            dma((levels, 6)), dma((levels, 6)), dma((levels, 6)), dma((levels, 6)),
            dma((levels, 6)), dma((levels, 6)), dma((levels, 6)), dma((levels, 6)),
            dma((4,)), dma((4,)), dma, dma,
            dma((4, 4)), dma((4,)), dma,
        ],
        compiler_params=pltpu.CompilerParams(
            collective_id=0, has_side_effects=True, vmem_limit_bytes=40 * 2**20
        ),
        cost_estimate=pl.CostEstimate(flops=flops, bytes_accessed=3 * tile * 4 * tile * 2, transcendentals=0),
    )(gain_mats, offsets, spread_mats)


def solution(mesh):
    in_specs = (P("tm", "row", None), P("tm", "row"), P("tm", "row", None))
    out_specs = (P("tm", "row"), P("tm", "row", None))
    return jax.shard_map(per_device, mesh=mesh, in_specs=in_specs, out_specs=out_specs, check_vma=False)
```

```python
import functools

import jax
import jax.numpy as jnp
from jax import lax
from jax.experimental import pallas as pl
from jax.experimental.pallas import tpu as pltpu
from jax.sharding import PartitionSpec as P

MESH = pl.DeviceIdType.MESH
BF16 = jnp.bfloat16
F32 = jnp.float32
PLAN = (
    "D0", "T0", "P0", "O0", "B00", "B01", "g00", "t00", "t01", "b0", "g01", "n0", "t02", "w0", "E0", "F10", "H1", "t03", "t04", "t05",
    "G10", "G11", "u00", "u01", "u02", "u03", "u04", "u05", "M0", "L0", "g10", "t10", "t11", "b1", "g11", "n1", "t12", "w1", "E1", "F20",
    "H2", "t13", "t14", "t15", "G20", "G21", "u10", "u11", "u12", "u13", "u14", "u15", "M1", "L1", "g20", "t20", "t21", "b2", "g21", "n2",
    "t22", "w2", "E2", "F30", "H3", "t23", "t24", "t25", "G30", "G31", "u20", "u21", "u22", "u23", "u24", "u25", "M2", "L2", "g30", "t30",
    "t31", "b3", "g31", "n3", "t32", "w3", "E3", "F40", "H4", "t33", "t34", "t35", "G40", "G41", "u30", "u31", "u32", "u33", "u34", "u35",
    "M3", "L3", "g40", "t40", "t41", "b4", "g41", "t42", "w4", "t43", "t44", "t45", "u40", "u41", "u42", "u43", "u44", "u45", "M4", "L4",
)
HALVES = 2
FARS = 1
PARTS = 2
SLAB = 16


def dot(a, b):
    return jnp.dot(a, b, preferred_element_type=F32)


def dot_t(a, b):
    return lax.dot_general(a, b, (((1,), (1,)), ((), ())), preferred_element_type=F32)


def kernel(
    steps, levels, tile,
    e_in, g_in, l_in, o_g, o_l,
    stage_e, stage_l, stage_g, e_first, e_later, far_e, far_l, far_g, own_l, own_g, mid, acc_e, fin_l, fin_g, offset_row,
    mve_s, mve_r, mvl_s, mvl_r, fed_s, fed_r, fe_s, fe_r, gd_s, gd_r, fgd_s, fgd_r, fg_s, fg_r,
    sib_s, sib_r, par_s, par_r, fwd_s, fwd_r,
    lf_s, lf_r, ls_s, ls_r, lp_s, lp_r, lw_s, lw_r, fin_s, fin_r, fing_s, fing_r, in_s, out_s, off_s,
):
    k = lax.axis_index("tm")
    y = lax.axis_index("row")
    core = k % 2
    column = k // 2
    parity = y // 2
    e = 2 * column + parity
    first = y + parity * (3 - 2 * y)
    q = first + core * (3 - 2 * first)
    q_sib = 3 - q
    q_par = q + 1 - 2 * (q % 2)
    q_dia = 3 - q_par
    sib = (k + 1 - 2 * core, y)
    par = (k, y + 1 - 2 * (y % 2))
    stays = parity == core
    moves = parity != core
    partner = (k + 1 - 2 * core, 3 - y)

    def holder(element, quarter):
        c = quarter // 2
        b = quarter + c * (3 - 2 * quarter)
        p = element % 2
        return (2 * (element // 2) + c, b + p * (3 - 2 * b))

    def copy(src, dst, ssem, rsem, dev):
        return pltpu.make_async_remote_copy(
            src_ref=src, dst_ref=dst, send_sem=ssem, recv_sem=rsem, device_id=dev, device_id_type=MESH
        )

    def composes(el, s):
        return el + 2**s < steps

    def makes_gain(el, s):
        return el + 2 ** (s + 1) < steps

    def sends_gain(el, s):
        return jnp.logical_and(el >= 2**s, el + 2**s < steps)

    def both(a, b):
        return jnp.logical_and(a, b)

    feeds_self = both(core == 1, y < 2)

    barrier = pltpu.get_barrier_semaphore()

    def greet(dev):
        pl.semaphore_signal(barrier, inc=1, device_id=dev, device_id_type=MESH)

    greet(sib)
    greet(par)
    for row in range(4):

        @pl.when(jnp.logical_not(both(stays, row == y)))
        def _():
            greet((e, row))

        @pl.when(both(e + 1 < steps, jnp.logical_not(both(feeds_self, row == y))))
        def _():
            greet((e + 1, row))

    for s in range(1, levels):

        @pl.when(composes(e, s))
        def _():
            greet((k + 2**s, y))

    def count(flag):
        return flag.astype(jnp.int32)

    greetings = 2 + 4 - count(stays) + count(k >= 1) * (4 - count(feeds_self))
    for s in range(1, levels):
        greetings += count(e >= 2**s)

    def blocks(s):
        return e_first if s == 0 else e_later.at[s - 1]

    def gain(s, a, b):
        return e_first[a, b] if s == 0 else e_later[s - 1, b, a]

    parts = PARTS
    tiles = 4 // parts

    def half(s, blk, h):
        return blocks(s).at[blk, pl.ds(tiles * h, tiles)]

    def gain_sib(s, h):
        return copy(half(s, q, h), half(s, q, h), sib_s.at[s, h], sib_r.at[s, h], sib)

    def gain_sib_in(s, h):
        return copy(half(s, q_sib, h), half(s, q_sib, h), sib_s.at[s, h], sib_r.at[s, h], sib)

    def gain_par(s, h):
        return copy(half(s, q, h), half(s, q, h), par_s.at[s, h], par_r.at[s, h], par)

    def gain_par_in(s, h):
        return copy(half(s, q_par, h), half(s, q_par, h), par_s.at[s, h], par_r.at[s, h], par)

    def gain_fwd(s, h):
        return copy(half(s, q_par, h), half(s, q_par, h), fwd_s.at[s, h], fwd_r.at[s, h], sib)

    def gain_fwd_in(s, h):
        return copy(half(s, q_dia, h), half(s, q_dia, h), fwd_s.at[s, h], fwd_r.at[s, h], sib)

    def gain_start(s, h):
        gain_par(s, h).start()

    def far_gain(s, h):
        part = pl.ds(h * (4 // FARS), 4 // FARS)
        return copy(e_later.at[s - 1, q, part], far_e.at[s, part], fe_s.at[s, h], fe_r.at[s, h], (k - 2**s, y))

    def far_offset(s):
        return copy(own_g, far_g.at[s], fg_s.at[s], fg_r.at[s], (k - 2**s, y))

    pieces = 3 * HALVES

    def rows(c):
        return pl.ds(c % HALVES * (tile // HALVES), tile // HALVES)

    def far_tile(s, c):
        t = c // HALVES
        return copy(
            own_l.at[(q + t) % 4, rows(c)], far_l.at[s, 3 * q + t, rows(c)], lf_s.at[s, c], lf_r.at[s, c], (k - 2**s, y)
        )

    def tile_copy(s, c, owner, ssem, rsem, dev):
        ref = far_l.at[s, 3 * owner + c // HALVES, rows(c)]
        return copy(ref, ref, ssem.at[s, c], rsem.at[s, c], dev)

    def tile_sib(s, t):
        return tile_copy(s, t, q, ls_s, ls_r, sib)

    def tile_sib_in(s, t):
        return tile_copy(s, t, q_sib, ls_s, ls_r, sib)

    def tile_par(s, t):
        return tile_copy(s, t, q, lp_s, lp_r, par)

    def tile_par_in(s, t):
        return tile_copy(s, t, q_par, lp_s, lp_r, par)

    def tile_fwd(s, t):
        return tile_copy(s, t, q_par, lw_s, lw_r, sib)

    def tile_fwd_in(s, t):
        return tile_copy(s, t, q_dia, lw_s, lw_r, sib)

    def if_tile(t, whose, run):
        if t < 2 * HALVES:
            run()
        else:
            pl.when(whose == 0)(run)

    def spread(s, a, b):
        t = (b - a) % 4
        if t < 2 or (t == 2 and a < 2):
            return far_l[s, 3 * a + t], False
        return far_l[s, 3 * b + (4 - t)], True

    def move_gain(h):
        part = pl.ds(tiles * h, tiles)
        return copy(stage_e.at[part], e_first.at[y, part], mve_s.at[h], mve_r.at[h], partner)

    def move_gain_in(h):
        part = pl.ds(tiles * h, tiles)
        return copy(stage_e.at[part], e_first.at[q, part], mve_s.at[h], mve_r.at[h], partner)

    def move_spread():
        return copy(stage_l, own_l, mvl_s, mvl_r, partner)

    def gain_direct(quarter):
        return copy(
            stage_e.at[quarter], far_e.at[0, y], fed_s.at[quarter], fed_r.at[y], holder(k - 1, quarter)
        )

    def gain_direct_in(row):
        return copy(stage_e.at[0], far_e.at[0, row], fed_s.at[row], fed_r.at[row], sib)

    def tile_direct(c):
        t = c // HALVES
        return copy(
            stage_l.at[(y + t) % 4, rows(c)], far_l.at[0, 3 * y + t, rows(c)], lf_s.at[0, c], lf_r.at[0, c],
            holder(k - 1, y),
        )

    def tile_in(s, c):
        return copy(own_l.at[0, rows(c)], far_l.at[s, 3 * q + c // HALVES, rows(c)], lf_s.at[s, c], lf_r.at[s, c], sib)

    def offset_direct(quarter):
        return copy(stage_g, own_g.at[y], gd_s.at[quarter], gd_r.at[y], holder(k, quarter))

    def offset_direct_in(row):
        return copy(stage_g, own_g.at[row], gd_s.at[row], gd_r.at[row], sib)

    def offset_direct_far(quarter):
        return copy(stage_g, far_g.at[0, y], fgd_s.at[quarter], fgd_r.at[y], holder(k - 1, quarter))

    def offset_direct_far_in(row):
        return copy(stage_g, far_g.at[0, row], fgd_s.at[row], fgd_r.at[row], sib)

    def load_gain(n):
        return pltpu.make_async_copy(e_in.at[0, :, pl.ds(n * tile, tile)], stage_e.at[n], in_s.at[0, n])

    def load_own_gain(n):
        return pltpu.make_async_copy(e_in.at[0, :, pl.ds(n * tile, tile)], e_first.at[q, n], in_s.at[1, n])

    def load_spread(n):
        return pltpu.make_async_copy(l_in.at[0, :, pl.ds(n * tile, tile)], stage_l.at[n], in_s.at[2, n])

    def load_own_spread(n):
        return pltpu.make_async_copy(l_in.at[0, :, pl.ds(n * tile, tile)], own_l.at[n], in_s.at[3, n])

    def store_own(n):
        return pltpu.make_async_copy(own_l.at[n], o_l.at[0, :, pl.ds(pl.multiple_of(n * tile, tile), tile)], out_s.at[n])

    def store_back(n):
        return pltpu.make_async_copy(fin_l.at[n], o_l.at[0, :, pl.ds(pl.multiple_of(n * tile, tile), tile)], out_s.at[n])

    def back(n):
        return copy(own_l.at[n], fin_l.at[n], fin_s.at[n], fin_r.at[n], partner)

    def back_offset():
        return copy(own_g.at[q], fin_g, fing_s, fing_r, partner)

    input_gain_sent = both(k >= 1, makes_gain(k - 1, 0))

    for n in range(4):
        load_spread(n).start()
    for n in range(4):
        load_gain(n).start()

    @pl.when(stays)
    def _():
        for n in range(4):
            load_own_gain(n).start()
        for n in range(4):
            load_own_spread(n).start()

    load_offset = pltpu.make_async_copy(g_in, offset_row, off_s)
    load_offset.start()
    load_offset.wait()
    first_row = lax.broadcasted_iota(jnp.int32, (SLAB, tile), 0) == 0
    slab = jnp.broadcast_to(offset_row[...].astype(F32), (SLAB, tile))
    stage_g[...] = jnp.where(first_row, slab, 0.0).astype(BF16)
    for n in range(4):
        load_spread(n).wait()
    for n in range(4):
        load_gain(n).wait()

    @pl.when(stays)
    def _():
        for n in range(4):
            load_own_gain(n).wait()

    pl.semaphore_wait(barrier, greetings)

    @pl.when(both(moves, composes(k, 0)))
    def _():
        for h in range(parts):
            move_gain(h).start()

    @pl.when(both(stays, composes(e, 0)))
    def _():
        for h in range(parts):
            gain_start(0, h)
        for h in range(parts):
            gain_sib(0, h).start()

    @pl.when(stays)
    def _():
        for n in range(4):
            load_own_spread(n).wait()

    def ring_moved(s, h):
        @pl.when(both(moves, composes(e, s)))
        def _():
            move_gain_in(h).wait_recv()
            gain_start(s, h)
            gain_sib(s, h).start()

    def tiles_direct(s):
        @pl.when(k >= 1)
        def _():
            for c in range(pieces):
                if_tile(c, y // 2, lambda c=c: tile_direct(c).start())

    def offsets_out(s):
        for quarter in range(4):
            here = both(stays, quarter == y)

            @pl.when(jnp.logical_not(here))
            def _():
                offset_direct(quarter).start()

            @pl.when(here)
            def _():
                own_g[y] = stage_g[...]

        @pl.when(k >= 1)
        def _():
            for quarter in range(4):
                here = both(feeds_self, quarter == 3 - y)

                @pl.when(jnp.logical_not(here))
                def _():
                    offset_direct_far(quarter).start()

                @pl.when(here)
                def _():
                    far_g[0, y] = stage_g[...]

    def spread_out(s):
        @pl.when(moves)
        def _():
            move_spread().start()

    def direct_out(s):
        @pl.when(input_gain_sent)
        def _():
            for quarter in range(4):
                here = both(feeds_self, quarter == 3 - y)

                @pl.when(jnp.logical_not(here))
                def _():
                    gain_direct(quarter).start()

                @pl.when(here)
                def _():
                    far_e[0, y] = stage_e[quarter]

    def ring_out(s, h):
        @pl.when(composes(e, s))
        def _():
            gain_start(s, h)

    def ring_near(s):
        @pl.when(composes(e, s))
        def _():
            for h in range(parts):
                gain_sib(s, h).start()

    def far_out(s, h):
        @pl.when(sends_gain(e, s))
        def _():
            far_gain(s, h).start()

    def ring_on(s, h):
        @pl.when(composes(e, s))
        def _():
            gain_par_in(s, h).wait_recv()
            gain_fwd(s, h).start()

    def tile_on(s, t):
        def run():
            tile_in(s, t).wait_recv()
            tile_par(s, t).start()
            tile_sib(s, t).start()

        @pl.when(composes(e, s))
        def _():
            if_tile(t, core, run)

    def tile_over(s, t):
        def run():
            tile_par_in(s, t).wait_recv()
            tile_fwd(s, t).start()

        @pl.when(composes(e, s))
        def _():
            if_tile(t, core, run)

    def gain_beside(s):
        @pl.when(composes(e, s))
        def _():
            for h in range(parts):
                gain_sib_in(s, h).wait_recv()

    def gain_near(s):
        @pl.when(makes_gain(e, s))
        def _():
            if s == 0:
                for row in range(4):

                    @pl.when(jnp.logical_not(both(feeds_self, row == y)))
                    def _():
                        gain_direct_in(row).wait_recv()

            else:
                for h in range(FARS):
                    far_gain(s, h).wait_recv()
                for a in range(4):
                    acc_e[a] = (
                        dot(gain(s, a, q), far_e[s, q])
                        + dot(gain(s, a, q_sib), far_e[s, q_sib])
                        + dot(gain(s, a, q_par), far_e[s, q_par])
                    )

    def gain_whole(s):
        @pl.when(composes(e, s))
        def _():
            for h in range(parts):
                gain_fwd_in(s, h).wait_recv()

    def gain_new(s):
        @pl.when(makes_gain(e, s))
        def _():
            for a in range(4):
                if s == 0:
                    total = dot(gain(s, a, 0), far_e[s, 0])
                    for b in range(1, 4):
                        total += dot(gain(s, a, b), far_e[s, b])
                else:
                    total = acc_e[a] + dot(gain(s, a, q_dia), far_e[s, q_dia])
                e_later[s, q, a] = total.astype(BF16)

    def middle(s):
        @pl.when(composes(e, s))
        def _():
            for t in range(pieces):

                def run(t=t):
                    tile_sib_in(s, t).wait_recv()
                    tile_fwd_in(s, t).wait_recv()

                if_tile(t, 1 - core, run)
            for n in range(4):
                total = None
                for b in range(4):
                    part, turned = spread(s, b, n)
                    term = (dot_t if turned else dot)(gain(s, q, b), part)
                    total = term if total is None else total + term
                mid[n, pl.ds(0, tile), :] = total.astype(BF16)
            if s == 0:
                for row in range(4):

                    @pl.when(jnp.logical_not(both(feeds_self, row == y)))
                    def _():
                        offset_direct_far_in(row).wait_recv()

            else:
                copy(far_g.at[s], far_g.at[s], fg_s.at[s], fg_r.at[s], sib).wait_recv()
            for b in range(4):
                mid[b, pl.ds(tile, SLAB), :] = far_g[s, b]

    def spread_new(s):
        more = s + 1 < levels
        if s == 0:

            @pl.when(moves)
            def _():
                move_spread().wait_recv()

            for row in range(4):

                @pl.when(jnp.logical_not(both(stays, row == y)))
                def _():
                    offset_direct_in(row).wait_recv()

        else:

            @pl.when(e >= 2**s)
            def _():
                for t in range(pieces):
                    if_tile(t, core, lambda t=t: far_tile(s, t).wait_send())
                far_offset(s).wait_send()

        @pl.when(composes(e, s))
        def _():
            for o in range(4):
                n = (q + o) % 4
                total = dot_t(mid[0], gain(s, n, 0))
                for b in range(1, 4):
                    total += dot_t(mid[b], gain(s, n, b))
                own_l[n] = (total[0:tile] + own_l[n].astype(F32)).astype(BF16)
                own_g[n] = (total[tile:] + own_g[n].astype(F32)).astype(BF16)
                if more:
                    if o < 3:

                        @pl.when(e >= 2 ** (s + 1))
                        def _():
                            for c in range(HALVES * o, HALVES * (o + 1)):
                                if_tile(c, core, lambda c=c: far_tile(s + 1, c).start())

                else:

                    @pl.when(moves)
                    def _():
                        back(n).start()

                    @pl.when(stays)
                    def _():
                        store_own(n).start()

        if more:

            @pl.when(both(e >= 2 ** (s + 1), jnp.logical_not(composes(e, s))))
            def _():
                for t in range(pieces):
                    if_tile(t, core, lambda t=t: far_tile(s + 1, t).start())

            @pl.when(e >= 2 ** (s + 1))
            def _():
                far_offset(s + 1).start()

        else:

            @pl.when(both(moves, jnp.logical_not(composes(e, s))))
            def _():
                for n in range(4):
                    back(n).start()

            @pl.when(both(stays, jnp.logical_not(composes(e, s))))
            def _():
                for n in range(4):
                    store_own(n).start()

    steps_of = dict(
        B=ring_moved, D=direct_out, T=tiles_direct, P=spread_out, O=offsets_out, b=gain_beside, G=ring_out, H=ring_near, F=far_out, g=ring_on, t=tile_on, u=tile_over, n=gain_near, w=gain_whole, E=gain_new, M=middle,
        L=spread_new,
    )
    for word in PLAN:
        args = [int(digit) for digit in word[1:]]
        steps_of[word[0]](*args)

    @pl.when(moves)
    def _():
        back_offset().start()
        for o in range(4):
            n = (y + o) % 4
            copy(own_l.at[n], fin_l.at[n], fin_s.at[n], fin_r.at[n], partner).wait_recv()
            store_back(n).start()
        back_offset().wait_recv()
        o_g[...] = fin_g[0:1]

    @pl.when(stays)
    def _():
        o_g[...] = own_g[q][0:1]

    for n in range(4):
        store_own(n).wait()
    @pl.when(moves)
    def _():
        back_offset().wait_send()
        for n in range(4):
            back(n).wait_send()
        move_spread().wait_send()

    @pl.when(both(moves, composes(k, 0)))
    def _():
        for h in range(parts):
            move_gain(h).wait_send()

    for quarter in range(4):
        here = both(feeds_self, quarter == 3 - y)

        @pl.when(both(input_gain_sent, jnp.logical_not(here)))
        def _():
            gain_direct(quarter).wait_send()

        @pl.when(both(k >= 1, jnp.logical_not(here)))
        def _():
            offset_direct_far(quarter).wait_send()

        @pl.when(jnp.logical_not(both(stays, quarter == y)))
        def _():
            offset_direct(quarter).wait_send()

    @pl.when(k >= 1)
    def _():
        for t in range(pieces):
            if_tile(t, y // 2, lambda t=t: tile_direct(t).wait_send())

    for s in range(levels):

        @pl.when(composes(e, s))
        def _():
            for h in range(parts):
                gain_par(s, h).wait_send()
                gain_sib(s, h).wait_send()
                gain_fwd(s, h).wait_send()
            for t in range(pieces):

                def run(t=t):
                    tile_par(s, t).wait_send()
                    tile_sib(s, t).wait_send()
                    tile_fwd(s, t).wait_send()

                if_tile(t, core, run)

        if s > 0:

            @pl.when(sends_gain(e, s))
            def _():
                for h in range(FARS):
                    far_gain(s, h).wait_send()


def per_device(gain_mats, offsets, spread_mats):
    steps = lax.axis_size("tm")
    levels = steps.bit_length() - 1
    tile = gain_mats.shape[1]
    dma = pltpu.SemaphoreType.DMA
    flops = levels * 3 * 2 * tile * (4 * tile) ** 2
    square = (tile, tile)
    return pl.pallas_call(
        functools.partial(kernel, steps, levels, tile),
        name="scan",
        out_shape=(
            jax.ShapeDtypeStruct(offsets.shape, BF16),
            jax.ShapeDtypeStruct(spread_mats.shape, BF16),
        ),
        in_specs=[pl.BlockSpec(memory_space=pltpu.HBM)] * 3,
        out_specs=[pl.BlockSpec(memory_space=pltpu.VMEM)] * 2,
        scratch_shapes=[
            pltpu.VMEM((4, *square), BF16),
            pltpu.VMEM((4, *square), BF16),
            pltpu.VMEM((SLAB, tile), BF16),
            pltpu.VMEM((4, 4, *square), BF16),
            pltpu.VMEM((levels - 1, 4, 4, *square), BF16),
            pltpu.VMEM((levels, 4, *square), BF16),
            pltpu.VMEM((levels, 12, *square), BF16),
            pltpu.VMEM((levels, 4, SLAB, tile), BF16),
            pltpu.VMEM((4, *square), BF16),
            pltpu.VMEM((4, SLAB, tile), BF16),
            pltpu.VMEM((4, tile + SLAB, tile), BF16),
            pltpu.VMEM((4, *square), F32),
            pltpu.VMEM((4, *square), BF16),
            pltpu.VMEM((SLAB, tile), BF16),
            pltpu.VMEM((1, tile), BF16),
            dma((4,)), dma((4,)), dma, dma,
            dma((4,)), dma((4,)), dma((levels, 4)), dma((levels, 4)),
            dma((4,)), dma((4,)), dma((4,)), dma((4,)), dma((levels,)), dma((levels,)),
            dma((levels, 4)), dma((levels, 4)), dma((levels, 4)), dma((levels, 4)), dma((levels, 4)), dma((levels, 4)),
            dma((levels, 6)), dma((levels, 6)), dma((levels, 6)), dma((levels, 6)),
            dma((levels, 6)), dma((levels, 6)), dma((levels, 6)), dma((levels, 6)),
            dma((4,)), dma((4,)), dma, dma,
            dma((4, 4)), dma((4,)), dma,
        ],
        compiler_params=pltpu.CompilerParams(
            collective_id=0, has_side_effects=True, vmem_limit_bytes=40 * 2**20
        ),
        cost_estimate=pl.CostEstimate(flops=flops, bytes_accessed=3 * tile * 4 * tile * 2, transcendentals=0),
    )(gain_mats, offsets, spread_mats)


def solution(mesh):
    in_specs = (P("tm", "row", None), P("tm", "row"), P("tm", "row", None))
    out_specs = (P("tm", "row"), P("tm", "row", None))
    return jax.shard_map(per_device, mesh=mesh, in_specs=in_specs, out_specs=out_specs, check_vma=False)
```

```python
import functools

import jax
import jax.numpy as jnp
from jax import lax
from jax.experimental import pallas as pl
from jax.experimental.pallas import tpu as pltpu
from jax.sharding import PartitionSpec as P

MESH = pl.DeviceIdType.MESH
BF16 = jnp.bfloat16
F32 = jnp.float32
PLAN = (
    "D0", "T0", "P0", "O0", "B00", "B01", "g00", "t00", "t01", "b0", "g01", "n0", "t02", "w0", "E0", "F10", "H1", "t03", "t04", "t05",
    "G10", "G11", "u00", "u01", "u02", "u03", "u04", "u05", "M0", "L0", "g10", "t10", "t11", "b1", "g11", "n1", "t12", "w1", "E1", "F20",
    "H2", "t13", "t14", "t15", "G20", "G21", "u10", "u11", "u12", "u13", "u14", "u15", "M1", "L1", "g20", "t20", "t21", "b2", "g21", "n2",
    "t22", "w2", "E2", "F30", "H3", "t23", "t24", "t25", "G30", "G31", "u20", "u21", "u22", "u23", "u24", "u25", "M2", "L2", "g30", "t30",
    "t31", "b3", "g31", "n3", "t32", "w3", "E3", "H4", "t33", "t34", "t35", "G40", "G41", "u30", "u31", "u32", "u33", "u34", "u35", "M3",
    "L3", "t40", "t41", "t42", "t43", "g40", "t44", "t45", "g41", "u40", "u41", "u42", "u43", "u44", "u45", "b4", "w4", "M4", "L4",
)
HALVES = 2
FARS = 1
PARTS = 2
SLAB = 16


def dot(a, b):
    return jnp.dot(a, b, preferred_element_type=F32)


def dot_t(a, b):
    return lax.dot_general(a, b, (((1,), (1,)), ((), ())), preferred_element_type=F32)


def kernel(
    steps, levels, tile,
    e_in, g_in, l_in, o_g, o_l,
    stage_e, stage_l, stage_g, e_first, e_later, far_e, far_l, far_g, own_l, own_g, mid, acc_e, fin_l, fin_g, offset_row,
    mve_s, mve_r, mvl_s, mvl_r, fed_s, fed_r, fe_s, fe_r, gd_s, gd_r, fgd_s, fgd_r, fg_s, fg_r,
    sib_s, sib_r, par_s, par_r, fwd_s, fwd_r,
    lf_s, lf_r, ls_s, ls_r, lp_s, lp_r, lw_s, lw_r, fin_s, fin_r, fing_s, fing_r, in_s, out_s, off_s,
):
    k = lax.axis_index("tm")
    y = lax.axis_index("row")
    core = k % 2
    column = k // 2
    parity = y // 2
    e = 2 * column + parity
    first = y + parity * (3 - 2 * y)
    q = first + core * (3 - 2 * first)
    q_sib = 3 - q
    q_par = q + 1 - 2 * (q % 2)
    q_dia = 3 - q_par
    sib = (k + 1 - 2 * core, y)
    par = (k, y + 1 - 2 * (y % 2))
    stays = parity == core
    moves = parity != core
    partner = (k + 1 - 2 * core, 3 - y)

    def holder(element, quarter):
        c = quarter // 2
        b = quarter + c * (3 - 2 * quarter)
        p = element % 2
        return (2 * (element // 2) + c, b + p * (3 - 2 * b))

    def copy(src, dst, ssem, rsem, dev):
        return pltpu.make_async_remote_copy(
            src_ref=src, dst_ref=dst, send_sem=ssem, recv_sem=rsem, device_id=dev, device_id_type=MESH
        )

    def composes(el, s):
        return el + 2**s < steps

    def makes_gain(el, s):
        return el + 2 ** (s + 1) < steps

    def sends_gain(el, s):
        return jnp.logical_and(el >= 2**s, el + 2**s < steps)

    def both(a, b):
        return jnp.logical_and(a, b)

    feeds_self = both(core == 1, y < 2)

    barrier = pltpu.get_barrier_semaphore()

    def greet(dev):
        pl.semaphore_signal(barrier, inc=1, device_id=dev, device_id_type=MESH)

    greet(sib)
    greet(par)
    for row in range(4):

        @pl.when(jnp.logical_not(both(stays, row == y)))
        def _():
            greet((e, row))

        @pl.when(both(e + 1 < steps, jnp.logical_not(both(feeds_self, row == y))))
        def _():
            greet((e + 1, row))

    for s in range(1, levels):

        @pl.when(composes(e, s))
        def _():
            greet((k + 2**s, y))

    def count(flag):
        return flag.astype(jnp.int32)

    greetings = 2 + 4 - count(stays) + count(k >= 1) * (4 - count(feeds_self))
    for s in range(1, levels):
        greetings += count(e >= 2**s)

    def blocks(s):
        return e_first if s == 0 else e_later.at[s - 1]

    def gain(s, a, b):
        return e_first[a, b] if s == 0 else e_later[s - 1, b, a]

    parts = PARTS
    tiles = 4 // parts

    def half(s, blk, h):
        return blocks(s).at[blk, pl.ds(tiles * h, tiles)]

    def gain_sib(s, h):
        return copy(half(s, q, h), half(s, q, h), sib_s.at[s, h], sib_r.at[s, h], sib)

    def gain_sib_in(s, h):
        return copy(half(s, q_sib, h), half(s, q_sib, h), sib_s.at[s, h], sib_r.at[s, h], sib)

    def gain_par(s, h):
        return copy(half(s, q, h), half(s, q, h), par_s.at[s, h], par_r.at[s, h], par)

    def gain_par_in(s, h):
        return copy(half(s, q_par, h), half(s, q_par, h), par_s.at[s, h], par_r.at[s, h], par)

    def gain_fwd(s, h):
        return copy(half(s, q_par, h), half(s, q_par, h), fwd_s.at[s, h], fwd_r.at[s, h], sib)

    def gain_fwd_in(s, h):
        return copy(half(s, q_dia, h), half(s, q_dia, h), fwd_s.at[s, h], fwd_r.at[s, h], sib)

    def gain_start(s, h):
        gain_par(s, h).start()

    def far_gain(s, h):
        part = pl.ds(h * (4 // FARS), 4 // FARS)
        return copy(e_later.at[s - 1, q, part], far_e.at[s, part], fe_s.at[s, h], fe_r.at[s, h], (k - 2**s, y))

    def far_offset(s):
        return copy(own_g, far_g.at[s], fg_s.at[s], fg_r.at[s], (k - 2**s, y))

    pieces = 3 * HALVES

    def rows(c):
        return pl.ds(c % HALVES * (tile // HALVES), tile // HALVES)

    def far_tile(s, c):
        t = c // HALVES
        return copy(
            own_l.at[(q + t) % 4, rows(c)], far_l.at[s, 3 * q + t, rows(c)], lf_s.at[s, c], lf_r.at[s, c], (k - 2**s, y)
        )

    def tile_copy(s, c, owner, ssem, rsem, dev):
        ref = far_l.at[s, 3 * owner + c // HALVES, rows(c)]
        return copy(ref, ref, ssem.at[s, c], rsem.at[s, c], dev)

    def tile_sib(s, t):
        return tile_copy(s, t, q, ls_s, ls_r, sib)

    def tile_sib_in(s, t):
        return tile_copy(s, t, q_sib, ls_s, ls_r, sib)

    def tile_par(s, t):
        return tile_copy(s, t, q, lp_s, lp_r, par)

    def tile_par_in(s, t):
        return tile_copy(s, t, q_par, lp_s, lp_r, par)

    def tile_fwd(s, t):
        return tile_copy(s, t, q_par, lw_s, lw_r, sib)

    def tile_fwd_in(s, t):
        return tile_copy(s, t, q_dia, lw_s, lw_r, sib)

    def if_tile(t, whose, run):
        if t < 2 * HALVES:
            run()
        else:
            pl.when(whose == 0)(run)

    def spread(s, a, b):
        t = (b - a) % 4
        if t < 2 or (t == 2 and a < 2):
            return far_l[s, 3 * a + t], False
        return far_l[s, 3 * b + (4 - t)], True

    def move_gain(h):
        part = pl.ds(tiles * h, tiles)
        return copy(stage_e.at[part], e_first.at[y, part], mve_s.at[h], mve_r.at[h], partner)

    def move_gain_in(h):
        part = pl.ds(tiles * h, tiles)
        return copy(stage_e.at[part], e_first.at[q, part], mve_s.at[h], mve_r.at[h], partner)

    def move_spread():
        return copy(stage_l, own_l, mvl_s, mvl_r, partner)

    def gain_direct(quarter):
        return copy(
            stage_e.at[quarter], far_e.at[0, y], fed_s.at[quarter], fed_r.at[y], holder(k - 1, quarter)
        )

    def gain_direct_in(row):
        return copy(stage_e.at[0], far_e.at[0, row], fed_s.at[row], fed_r.at[row], sib)

    def tile_direct(c):
        t = c // HALVES
        return copy(
            stage_l.at[(y + t) % 4, rows(c)], far_l.at[0, 3 * y + t, rows(c)], lf_s.at[0, c], lf_r.at[0, c],
            holder(k - 1, y),
        )

    def tile_in(s, c):
        return copy(own_l.at[0, rows(c)], far_l.at[s, 3 * q + c // HALVES, rows(c)], lf_s.at[s, c], lf_r.at[s, c], sib)

    def offset_direct(quarter):
        return copy(stage_g, own_g.at[y], gd_s.at[quarter], gd_r.at[y], holder(k, quarter))

    def offset_direct_in(row):
        return copy(stage_g, own_g.at[row], gd_s.at[row], gd_r.at[row], sib)

    def offset_direct_far(quarter):
        return copy(stage_g, far_g.at[0, y], fgd_s.at[quarter], fgd_r.at[y], holder(k - 1, quarter))

    def offset_direct_far_in(row):
        return copy(stage_g, far_g.at[0, row], fgd_s.at[row], fgd_r.at[row], sib)

    def load_gain(n):
        return pltpu.make_async_copy(e_in.at[0, :, pl.ds(n * tile, tile)], stage_e.at[n], in_s.at[0, n])

    def load_own_gain(n):
        return pltpu.make_async_copy(e_in.at[0, :, pl.ds(n * tile, tile)], e_first.at[q, n], in_s.at[1, n])

    def load_spread(n):
        return pltpu.make_async_copy(l_in.at[0, :, pl.ds(n * tile, tile)], stage_l.at[n], in_s.at[2, n])

    def load_own_spread(n):
        return pltpu.make_async_copy(l_in.at[0, :, pl.ds(n * tile, tile)], own_l.at[n], in_s.at[3, n])

    def store_own(n):
        return pltpu.make_async_copy(own_l.at[n], o_l.at[0, :, pl.ds(pl.multiple_of(n * tile, tile), tile)], out_s.at[n])

    def store_back(n):
        return pltpu.make_async_copy(fin_l.at[n], o_l.at[0, :, pl.ds(pl.multiple_of(n * tile, tile), tile)], out_s.at[n])

    def back(n):
        return copy(own_l.at[n], fin_l.at[n], fin_s.at[n], fin_r.at[n], partner)

    def back_offset():
        return copy(own_g.at[q], fin_g, fing_s, fing_r, partner)

    input_gain_sent = both(k >= 1, makes_gain(k - 1, 0))

    for n in range(4):
        load_spread(n).start()
    for n in range(4):
        load_gain(n).start()

    @pl.when(stays)
    def _():
        for n in range(4):
            load_own_gain(n).start()
        for n in range(4):
            load_own_spread(n).start()

    load_offset = pltpu.make_async_copy(g_in, offset_row, off_s)
    load_offset.start()
    load_offset.wait()
    first_row = lax.broadcasted_iota(jnp.int32, (SLAB, tile), 0) == 0
    slab = jnp.broadcast_to(offset_row[...].astype(F32), (SLAB, tile))
    stage_g[...] = jnp.where(first_row, slab, 0.0).astype(BF16)
    for n in range(4):
        load_spread(n).wait()
    for n in range(4):
        load_gain(n).wait()

    @pl.when(stays)
    def _():
        for n in range(4):
            load_own_gain(n).wait()

    pl.semaphore_wait(barrier, greetings)

    @pl.when(both(moves, composes(k, 0)))
    def _():
        for h in range(parts):
            move_gain(h).start()

    @pl.when(both(stays, composes(e, 0)))
    def _():
        for h in range(parts):
            gain_start(0, h)
        for h in range(parts):
            gain_sib(0, h).start()

    @pl.when(stays)
    def _():
        for n in range(4):
            load_own_spread(n).wait()

    def ring_moved(s, h):
        @pl.when(both(moves, composes(e, s)))
        def _():
            move_gain_in(h).wait_recv()
            gain_start(s, h)
            gain_sib(s, h).start()

    def tiles_direct(s):
        @pl.when(k >= 1)
        def _():
            for c in range(pieces):
                if_tile(c, y // 2, lambda c=c: tile_direct(c).start())

    def offsets_out(s):
        for quarter in range(4):
            here = both(stays, quarter == y)

            @pl.when(jnp.logical_not(here))
            def _():
                offset_direct(quarter).start()

            @pl.when(here)
            def _():
                own_g[y] = stage_g[...]

        @pl.when(k >= 1)
        def _():
            for quarter in range(4):
                here = both(feeds_self, quarter == 3 - y)

                @pl.when(jnp.logical_not(here))
                def _():
                    offset_direct_far(quarter).start()

                @pl.when(here)
                def _():
                    far_g[0, y] = stage_g[...]

    def spread_out(s):
        @pl.when(moves)
        def _():
            move_spread().start()

    def direct_out(s):
        @pl.when(input_gain_sent)
        def _():
            for quarter in range(4):
                here = both(feeds_self, quarter == 3 - y)

                @pl.when(jnp.logical_not(here))
                def _():
                    gain_direct(quarter).start()

                @pl.when(here)
                def _():
                    far_e[0, y] = stage_e[quarter]

    def ring_out(s, h):
        @pl.when(composes(e, s))
        def _():
            gain_start(s, h)

    def ring_near(s):
        @pl.when(composes(e, s))
        def _():
            for h in range(parts):
                gain_sib(s, h).start()

    def far_out(s, h):
        @pl.when(sends_gain(e, s))
        def _():
            far_gain(s, h).start()

    def ring_on(s, h):
        @pl.when(composes(e, s))
        def _():
            gain_par_in(s, h).wait_recv()
            gain_fwd(s, h).start()

    def tile_on(s, t):
        def run():
            tile_in(s, t).wait_recv()
            tile_par(s, t).start()
            tile_sib(s, t).start()

        @pl.when(composes(e, s))
        def _():
            if_tile(t, core, run)

    def tile_over(s, t):
        def run():
            tile_par_in(s, t).wait_recv()
            tile_fwd(s, t).start()

        @pl.when(composes(e, s))
        def _():
            if_tile(t, core, run)

    def gain_beside(s):
        @pl.when(composes(e, s))
        def _():
            for h in range(parts):
                gain_sib_in(s, h).wait_recv()

    def gain_near(s):
        @pl.when(makes_gain(e, s))
        def _():
            if s == 0:
                for row in range(4):

                    @pl.when(jnp.logical_not(both(feeds_self, row == y)))
                    def _():
                        gain_direct_in(row).wait_recv()

            else:
                for h in range(FARS):
                    far_gain(s, h).wait_recv()
                for a in range(4):
                    acc_e[a] = (
                        dot(gain(s, a, q), far_e[s, q])
                        + dot(gain(s, a, q_sib), far_e[s, q_sib])
                        + dot(gain(s, a, q_par), far_e[s, q_par])
                    )

    def gain_whole(s):
        @pl.when(composes(e, s))
        def _():
            for h in range(parts):
                gain_fwd_in(s, h).wait_recv()

    def gain_new(s):
        @pl.when(makes_gain(e, s))
        def _():
            for a in range(4):
                if s == 0:
                    total = dot(gain(s, a, 0), far_e[s, 0])
                    for b in range(1, 4):
                        total += dot(gain(s, a, b), far_e[s, b])
                else:
                    total = acc_e[a] + dot(gain(s, a, q_dia), far_e[s, q_dia])
                e_later[s, q, a] = total.astype(BF16)

    def middle(s):
        @pl.when(composes(e, s))
        def _():
            for t in range(pieces):

                def run(t=t):
                    tile_sib_in(s, t).wait_recv()
                    tile_fwd_in(s, t).wait_recv()

                if_tile(t, 1 - core, run)
            for n in range(4):
                total = None
                for b in range(4):
                    part, turned = spread(s, b, n)
                    term = (dot_t if turned else dot)(gain(s, q, b), part)
                    total = term if total is None else total + term
                mid[n, pl.ds(0, tile), :] = total.astype(BF16)
            if s == 0:
                for row in range(4):

                    @pl.when(jnp.logical_not(both(feeds_self, row == y)))
                    def _():
                        offset_direct_far_in(row).wait_recv()

            else:
                copy(far_g.at[s], far_g.at[s], fg_s.at[s], fg_r.at[s], sib).wait_recv()
            for b in range(4):
                mid[b, pl.ds(tile, SLAB), :] = far_g[s, b]

    def spread_new(s):
        more = s + 1 < levels
        if s == 0:

            @pl.when(moves)
            def _():
                move_spread().wait_recv()

            for row in range(4):

                @pl.when(jnp.logical_not(both(stays, row == y)))
                def _():
                    offset_direct_in(row).wait_recv()

        else:

            @pl.when(e >= 2**s)
            def _():
                for t in range(pieces):
                    if_tile(t, core, lambda t=t: far_tile(s, t).wait_send())
                far_offset(s).wait_send()

        @pl.when(composes(e, s))
        def _():
            for o in range(4):
                n = (q + o) % 4
                total = dot_t(mid[0], gain(s, n, 0))
                for b in range(1, 4):
                    total += dot_t(mid[b], gain(s, n, b))
                own_l[n] = (total[0:tile] + own_l[n].astype(F32)).astype(BF16)
                own_g[n] = (total[tile:] + own_g[n].astype(F32)).astype(BF16)
                if more:
                    if o < 3:

                        @pl.when(e >= 2 ** (s + 1))
                        def _():
                            for c in range(HALVES * o, HALVES * (o + 1)):
                                if_tile(c, core, lambda c=c: far_tile(s + 1, c).start())

                else:

                    @pl.when(moves)
                    def _():
                        back(n).start()

                    @pl.when(stays)
                    def _():
                        store_own(n).start()

        if more:

            @pl.when(both(e >= 2 ** (s + 1), jnp.logical_not(composes(e, s))))
            def _():
                for t in range(pieces):
                    if_tile(t, core, lambda t=t: far_tile(s + 1, t).start())

            @pl.when(e >= 2 ** (s + 1))
            def _():
                far_offset(s + 1).start()

        else:

            @pl.when(both(moves, jnp.logical_not(composes(e, s))))
            def _():
                for n in range(4):
                    back(n).start()

            @pl.when(both(stays, jnp.logical_not(composes(e, s))))
            def _():
                for n in range(4):
                    store_own(n).start()

    steps_of = dict(
        B=ring_moved, D=direct_out, T=tiles_direct, P=spread_out, O=offsets_out, b=gain_beside, G=ring_out, H=ring_near, F=far_out, g=ring_on, t=tile_on, u=tile_over, n=gain_near, w=gain_whole, E=gain_new, M=middle,
        L=spread_new,
    )
    for word in PLAN:
        args = [int(digit) for digit in word[1:]]
        steps_of[word[0]](*args)

    @pl.when(moves)
    def _():
        back_offset().start()
        for o in range(4):
            n = (y + o) % 4
            copy(own_l.at[n], fin_l.at[n], fin_s.at[n], fin_r.at[n], partner).wait_recv()
            store_back(n).start()
        back_offset().wait_recv()
        o_g[...] = fin_g[0:1]

    @pl.when(stays)
    def _():
        o_g[...] = own_g[q][0:1]

    for n in range(4):
        store_own(n).wait()
    @pl.when(moves)
    def _():
        back_offset().wait_send()
        for n in range(4):
            back(n).wait_send()
        move_spread().wait_send()

    @pl.when(both(moves, composes(k, 0)))
    def _():
        for h in range(parts):
            move_gain(h).wait_send()

    for quarter in range(4):
        here = both(feeds_self, quarter == 3 - y)

        @pl.when(both(input_gain_sent, jnp.logical_not(here)))
        def _():
            gain_direct(quarter).wait_send()

        @pl.when(both(k >= 1, jnp.logical_not(here)))
        def _():
            offset_direct_far(quarter).wait_send()

        @pl.when(jnp.logical_not(both(stays, quarter == y)))
        def _():
            offset_direct(quarter).wait_send()

    @pl.when(k >= 1)
    def _():
        for t in range(pieces):
            if_tile(t, y // 2, lambda t=t: tile_direct(t).wait_send())

    for s in range(levels):

        @pl.when(composes(e, s))
        def _():
            for h in range(parts):
                gain_par(s, h).wait_send()
                gain_sib(s, h).wait_send()
                gain_fwd(s, h).wait_send()
            for t in range(pieces):

                def run(t=t):
                    tile_par(s, t).wait_send()
                    tile_sib(s, t).wait_send()
                    tile_fwd(s, t).wait_send()

                if_tile(t, core, run)

        if s > 0:

            @pl.when(sends_gain(e, s))
            def _():
                for h in range(FARS):
                    far_gain(s, h).wait_send()


def per_device(gain_mats, offsets, spread_mats):
    steps = lax.axis_size("tm")
    levels = steps.bit_length() - 1
    tile = gain_mats.shape[1]
    dma = pltpu.SemaphoreType.DMA
    flops = levels * 3 * 2 * tile * (4 * tile) ** 2
    square = (tile, tile)
    return pl.pallas_call(
        functools.partial(kernel, steps, levels, tile),
        name="scan",
        out_shape=(
            jax.ShapeDtypeStruct(offsets.shape, BF16),
            jax.ShapeDtypeStruct(spread_mats.shape, BF16),
        ),
        in_specs=[pl.BlockSpec(memory_space=pltpu.HBM)] * 3,
        out_specs=[pl.BlockSpec(memory_space=pltpu.VMEM)] * 2,
        scratch_shapes=[
            pltpu.VMEM((4, *square), BF16),
            pltpu.VMEM((4, *square), BF16),
            pltpu.VMEM((SLAB, tile), BF16),
            pltpu.VMEM((4, 4, *square), BF16),
            pltpu.VMEM((levels - 1, 4, 4, *square), BF16),
            pltpu.VMEM((levels, 4, *square), BF16),
            pltpu.VMEM((levels, 12, *square), BF16),
            pltpu.VMEM((levels, 4, SLAB, tile), BF16),
            pltpu.VMEM((4, *square), BF16),
            pltpu.VMEM((4, SLAB, tile), BF16),
            pltpu.VMEM((4, tile + SLAB, tile), BF16),
            pltpu.VMEM((4, *square), F32),
            pltpu.VMEM((4, *square), BF16),
            pltpu.VMEM((SLAB, tile), BF16),
            pltpu.VMEM((1, tile), BF16),
            dma((4,)), dma((4,)), dma, dma,
            dma((4,)), dma((4,)), dma((levels, 4)), dma((levels, 4)),
            dma((4,)), dma((4,)), dma((4,)), dma((4,)), dma((levels,)), dma((levels,)),
            dma((levels, 4)), dma((levels, 4)), dma((levels, 4)), dma((levels, 4)), dma((levels, 4)), dma((levels, 4)),
            dma((levels, 6)), dma((levels, 6)), dma((levels, 6)), dma((levels, 6)),
            dma((levels, 6)), dma((levels, 6)), dma((levels, 6)), dma((levels, 6)),
            dma((4,)), dma((4,)), dma, dma,
            dma((4, 4)), dma((4,)), dma,
        ],
        compiler_params=pltpu.CompilerParams(
            collective_id=0, has_side_effects=True, vmem_limit_bytes=40 * 2**20
        ),
        cost_estimate=pl.CostEstimate(flops=flops, bytes_accessed=3 * tile * 4 * tile * 2, transcendentals=0),
    )(gain_mats, offsets, spread_mats)


def solution(mesh):
    in_specs = (P("tm", "row", None), P("tm", "row"), P("tm", "row", None))
    out_specs = (P("tm", "row"), P("tm", "row", None))
    return jax.shard_map(per_device, mesh=mesh, in_specs=in_specs, out_specs=out_specs, check_vma=False)
```
